32 devices in a mesh: dp: 8 (over z, y), band: 4 (over x, core).
Axes of the slice: x: 2, y: 2, z: 4, core: 2. Of those that a mesh axis runs over, the one named last changes fastest.
Arguments:
- cell_states: bfloat16 [16, 32, 128, 768], P('dp', 'band'), may hold values from -6 to 6
- head_grads: bfloat16 [16, 32, 128, 384], P('dp', 'band'), may hold values from -6 to 6
- group_ids: int32 [16, 128, 32], P('dp', 'band'), may hold values from 0 to 7, never falling along the last dimension, each value on 1 to 8 neighbouring positions
- proj_weights: bfloat16 [768, 1152], replicated, may hold values from -0.8694895 to 0.8694895
Outputs:
- input_grad: bfloat16 [16, 32, 128, 768], P('dp', 'band')
- weight_grad: float32 [768, 1152], P('band', 'dp')
The draws below stay inside these ranges and needn't reach their ends.
Inputs may be any that keep to these rules, and one draw needn't show every extreme that they name: `group_ids`: group numbers never fall down the rows of a column; a cell sees the header row 0 and the cells of its own group.
All inputs are finite; a program needn't handle non-finite values.
Results may differ from the reference program's by a relative error of at most 0.008.
Values may be sent and summed in bfloat16 or wider, within the bound.
A program may use at most 128 MiB of HBM per device.

```python
import math
import jax
import jax.numpy as jnp
import numpy as np
from jax import lax

D = 768
HEADS = 6
HD = 64
ROWS = 32
COLS = 128
TABLES = 16
HA = 384


def draw_proj_weights(key, part):
    width = HEADS * HD
    base = jnp.clip(jax.random.normal(key, (D, 3 * width), jnp.float32), -4.0, 4.0) * D ** (-0.5)
    return base.astype(jnp.bfloat16)


def strengthened(drawn, key, source, target, parts, factor):
    def block_of(dim):
        return (jnp.arange(drawn.shape[dim]) // (drawn.shape[dim] // parts)).reshape((-1,) + (1,) * (drawn.ndim - 1 - dim))

    one_side = jax.random.permutation(key, parts)[block_of(target)]
    second = (block_of(target) + parts // 2) % parts
    return jnp.where((block_of(source) == one_side) | (block_of(source) == second), factor * drawn, drawn)


def block_levels(key, shape, shards, smallest, top_value):
    loudness, own = 1.0, jax.random.fold_in(key, 6)
    for axis_at, blocks in shards:
        draws = jnp.exp(jax.random.uniform(jax.random.fold_in(own, axis_at), (blocks,), jnp.float32, smallest / len(shards), top_value / len(shards)))
        loudness = loudness * jnp.repeat(draws, shape[axis_at] // blocks).reshape([-1 if axis == axis_at else 1 for axis in range(len(shape))])
    return loudness


def split_up(amount, total, bound, lean):
    portions = [(1 << 20) // math.isqrt(standing ** lean) + 1 for standing in range(2, amount + 1)]
    spare, counts = total - bound - (amount - 1), [1] * (amount - 1)
    while spare > 0:
        movable = [i for i in range(amount - 1) if counts[i] < bound]
        pool, left = sum([portions[i] for i in movable]), spare
        for i in movable:
            extra = min(bound - counts[i], max(1, left * portions[i] // pool), spare)
            counts[i] = counts[i] + extra
            spare = spare - extra
    return np.array([bound] + counts)


def ragged(own_key, number_of, total, most, skew):
    if number_of == 2:
        one = jax.random.randint(own_key, (), max(1, total - most), min(most, total - 1) + 1)
        return jnp.stack([one, total - one])
    lengths = jnp.asarray(split_up(number_of, total, most, skew), jnp.int32)
    pairs = (number_of - 1) // 2
    source_of, sink = lengths[1:1 + 2 * pairs:2], lengths[2:2 + 2 * pairs:2]
    room = jnp.minimum(source_of - 1, most - sink)
    passed = jax.random.randint(jax.random.fold_in(own_key, 1), (pairs,), 0, 1 << 20) % (room + 1)
    lengths = lengths.at[1:1 + 2 * pairs:2].set(source_of - passed).at[2:2 + 2 * pairs:2].set(sink + passed)
    return lengths[jax.random.permutation(jax.random.fold_in(own_key, 2), number_of)]


def bell_draw(stream_key, shape, spread, bound, cuts=(), kind=jnp.bfloat16):
    drawn = spread * jax.random.normal(stream_key, shape, jnp.float32)
    if cuts:
        drawn = drawn * block_levels(stream_key, shape, cuts, -0.22, 0.18)
    return jnp.clip(drawn, -bound, bound).astype(kind)


def heavy_noise(own_key, shape, deviation, most, cuts, heavy, kind=jnp.bfloat16):
    result = deviation * jax.random.normal(own_key, shape, jnp.float32)
    if cuts:
        result = result * block_levels(own_key, shape, cuts, -0.22, 0.18)
    return jnp.clip(strengthened(result, jax.random.fold_in(own_key, 3), *heavy), -most, most).astype(kind)


def setup_inputs(seed: int = 0) -> dict:
    seeds = jax.random.split(jax.random.key(seed), 5)
    cell_states = heavy_noise(seeds[0], (TABLES, ROWS, COLS, D), 1.0, 6.0, ((0, 8), (1, 4)), (1, 3, 4, 2.0))
    head_grads = bell_draw(seeds[1], (TABLES, ROWS, COLS, HA), 1.0, 6.0, ((0, 8), (1, 4)))
    group_ids = jax.vmap(lambda own: jnp.searchsorted(jnp.cumsum(ragged(own, 8, ROWS, 8, 2)), jnp.arange(ROWS), side="right"))(jax.random.split(seeds[2], TABLES * COLS)).reshape((TABLES, COLS, ROWS)).astype(jnp.int32)
    proj_weights = draw_proj_weights(jax.random.fold_in(seeds[4], 71), 0)
    return dict(cell_states=cell_states, head_grads=head_grads, group_ids=group_ids, proj_weights=proj_weights)


SCALE = 0.125
EPSILON = 1e-06

def normalize(states):
    widened = states.astype(jnp.float32)
    meansq = lax.optimization_barrier(jnp.mean(widened * widened, axis=-1, keepdims=True))
    inverse = lax.rsqrt(meansq + EPSILON)
    scaled = widened * inverse
    return (scaled, inverse, scaled.astype(jnp.bfloat16))

def project(normed, weights):
    width = weights.shape[1] // 3
    flat = normed.reshape(-1, normed.shape[-1])
    mixed = jnp.dot(flat, weights, preferred_element_type=jnp.float32).astype(jnp.bfloat16)
    mixed = mixed.reshape(normed.shape[:-1] + (3 * width,))
    return (mixed[..., :width], mixed[..., width:2 * width], mixed[..., 2 * width:])

def attend_back(query_rows, key_rows, value_rows, grad_rows, groups):
    shape = query_rows.shape
    split = shape[:-1] + (shape[-1] // HD, HD)
    query_five = query_rows.reshape(split).astype(jnp.float32)
    key_five = key_rows.reshape(split).astype(jnp.float32)
    value_five = value_rows.reshape(split).astype(jnp.float32)
    grad_five = grad_rows.reshape(split).astype(jnp.float32)
    scores = jnp.einsum('bichd,bjchd->bchij', query_five, key_five) * SCALE
    header = lax.broadcasted_iota(jnp.int32, (shape[1], shape[1]), 1) == 0
    visible = (groups[:, :, :, None] == groups[:, :, None, :]) | header
    scores = jnp.where(visible[:, :, None], scores, -1e+30)
    peak = lax.optimization_barrier(jnp.max(scores, axis=-1, keepdims=True))
    expsc = jnp.exp(scores - peak)
    probs = expsc / lax.optimization_barrier(jnp.sum(expsc, axis=-1, keepdims=True))
    probs_low = probs.astype(jnp.bfloat16).astype(jnp.float32)
    value_grad = jnp.einsum('bchij,bichd->bjchd', probs_low, grad_five).astype(jnp.bfloat16)
    prob_grad = jnp.einsum('bichd,bjchd->bchij', grad_five, value_five)
    score_grad = probs * (prob_grad - lax.optimization_barrier(jnp.sum(probs * prob_grad, axis=-1, keepdims=True)))
    score_low = (score_grad * SCALE).astype(jnp.bfloat16).astype(jnp.float32)
    query_grad = jnp.einsum('bchij,bjchd->bichd', score_low, key_five).astype(jnp.bfloat16)
    key_grad = jnp.einsum('bchij,bichd->bjchd', score_low, query_five).astype(jnp.bfloat16)
    return (query_grad.reshape(shape), key_grad.reshape(shape), value_grad.reshape(shape))

def finish(scaled, inverse, normed, all_grads, weights):
    flat_norm = normed.reshape(-1, normed.shape[-1])
    flat_grad = all_grads.reshape(-1, all_grads.shape[-1])
    partial_w = jnp.dot(flat_norm.T, flat_grad, preferred_element_type=jnp.float32)
    normed_grad = jnp.dot(flat_grad, weights.T, preferred_element_type=jnp.float32).reshape(scaled.shape)
    coupling = lax.optimization_barrier(jnp.mean(normed_grad * scaled, axis=-1, keepdims=True))
    state_grad = (inverse * (normed_grad - scaled * coupling)).astype(jnp.bfloat16)
    return (partial_w, state_grad)

def reference(cell_states, head_grads, group_ids, proj_weights):

    def one_table(total, pieces):
        states, grads, groups = pieces
        scaled, inverse, normed = normalize(states)
        query_rows, key_rows, value_rows = project(normed, proj_weights)
        query_grad, key_grad, value_grad = attend_back(query_rows[None], key_rows[None], value_rows[None], grads[None], groups[None])
        all_grads = jnp.concatenate((query_grad, key_grad, value_grad), axis=-1)[0]
        partial_w, state_grad = finish(scaled, inverse, normed, all_grads, proj_weights)
        return (total + partial_w, state_grad)
    start = jnp.zeros((D, 3 * HEADS * HD), jnp.float32)
    total, input_grad = lax.scan(one_table, start, (cell_states, head_grads, group_ids))
    return (input_grad, total)
```

```python
import functools

import jax
import jax.numpy as jnp
from jax import lax
from jax.experimental import pallas as pl
from jax.experimental.pallas import tpu as pltpu
from jax.sharding import PartitionSpec as P

HD = 64
SCALE = 0.125
EPSILON = 1e-06
LOW = 4
HIGH = 3
BAND = 8
SLOTS = 1 + LOW + BAND + HIGH
SUB = 8
STEP = 16
CELLS = SLOTS * SUB
F32 = jnp.float32
BF16 = jnp.bfloat16


def dot(a, b, ca, cb):
    return lax.dot_general(a, b, (((ca,), (cb,)), ((), ())), preferred_element_type=F32)


def split_heads(a):
    left = lax.broadcasted_iota(jnp.int32, a.shape, 1) < HD
    zero = jnp.zeros_like(a)
    return jnp.concatenate((jnp.where(left, a, zero), jnp.where(left, zero, a)), axis=0)


def kernel(first, *refs):
    if first:
        code, hx, lx, ox, ux, lg, og, ug, w, out_h, out_l, out_o, out_u, wg, mixed, grads = refs
    else:
        code, hx, lx, ox, ux, lg, og, ug, w, wg_in, out_h, out_l, out_o, out_u, wg, mixed, grads = refs
    width = og.shape[-1]

    def flat(parts):
        whole = jnp.concatenate(parts, axis=0).astype(F32)
        return jnp.concatenate(
            [whole[:, s : s + SUB].reshape(CELLS, whole.shape[-1]) for s in range(0, STEP, SUB)], axis=0
        )

    states = flat((hx[0], lx[0], ox[0], ux[0]))
    inverse = lax.rsqrt(jnp.mean(states * states, axis=-1, keepdims=True) + EPSILON)
    scaled = states * inverse
    normed = scaled.astype(BF16)
    mixed[...] = dot(normed, w[...], 1, 0).astype(BF16)
    cotangent = flat((jnp.zeros((1, STEP, width), BF16), lg[0], og[0], ug[0])).astype(BF16)

    for s in range(STEP // SUB):
        rows = slice(s * CELLS, (s + 1) * CELLS)
        query_code = code[0, 0, s : s + 1, :]
        key_code = jnp.broadcast_to(code[0, 0, s + 2 : s + 3, :], (CELLS, CELLS)).T
        query_column = query_code >> 3
        at = lax.broadcasted_iota(jnp.int32, (CELLS, CELLS), 0)
        visible = (key_code == query_code) | (at == query_column)
        bias = jnp.where(visible, 0.0, -1e30).astype(F32)
        for p in range(width // 128):
            lanes = slice(128 * p, 128 * p + 128)
            query = mixed[rows, lanes] * jnp.asarray(SCALE, BF16)
            key = mixed[rows, width + 128 * p : width + 128 * p + 128]
            value = mixed[rows, 2 * width + 128 * p : 2 * width + 128 * p + 128]
            grad = cotangent[rows, lanes]
            scores = dot(split_heads(key), query, 1, 1).reshape(2, CELLS, CELLS) + bias[None]
            peak = jnp.maximum(jnp.max(scores, axis=1, keepdims=True), -1e29)
            expsc = jnp.exp(scores - peak)
            total = jnp.maximum(jnp.sum(expsc, axis=1, keepdims=True), 1.0)
            probs = expsc * (1.0 / total)
            prob_grad = dot(split_heads(value), grad, 1, 1).reshape(2, CELLS, CELLS)
            delta = jnp.sum(probs * prob_grad, axis=1, keepdims=True)
            score_low = (probs * (prob_grad - delta)).astype(BF16)
            probs_low = probs.astype(BF16)
            value_grad = dot(
                jnp.concatenate((probs_low[0], probs_low[1]), axis=1), split_heads(grad), 1, 0
            )
            key_grad = dot(
                jnp.concatenate((score_low[0], score_low[1]), axis=1), split_heads(query), 1, 0
            )
            query_grad = dot(
                score_low.reshape(2 * CELLS, CELLS), split_heads(key * jnp.asarray(SCALE, BF16)), 0, 0
            )
            grads[rows, lanes] = query_grad.astype(BF16)
            grads[rows, width + 128 * p : width + 128 * p + 128] = key_grad.astype(BF16)
            grads[rows, 2 * width + 128 * p : 2 * width + 128 * p + 128] = value_grad.astype(BF16)

    normed_grad = dot(grads[...], w[...], 1, 1)
    coupling = jnp.mean(normed_grad * scaled, axis=-1, keepdims=True)
    result = inverse * (normed_grad - scaled * coupling)
    parts = [result[s * CELLS : (s + 1) * CELLS].reshape(SLOTS, SUB, -1) for s in range(STEP // SUB)]
    result = jnp.concatenate(parts, axis=1).astype(BF16)
    out_h[0] = result[:1]
    out_l[0] = result[1 : 1 + LOW]
    out_o[0] = result[1 + LOW : 1 + LOW + BAND]
    out_u[0] = result[1 + LOW + BAND :]

    term = dot(normed, grads[...], 0, 0)

    @pl.when(pl.program_id(0) == 0)
    def _():
        wg[...] = term if first else wg_in[...] + term

    @pl.when(pl.program_id(0) != 0)
    def _():
        wg[...] += term


def attend(code, states, cots, weights, earlier):
    cols, wide = states[2].shape[2:]
    width = cots[1].shape[-1]

    def block(rows, features):
        return pl.BlockSpec((1, rows, STEP, features), lambda i: (0, 0, i, 0))

    whole = lambda shape: pl.BlockSpec(shape, lambda i: (0,) * len(shape))
    in_specs = [pl.BlockSpec((1, 1, 2 * STEP // SUB, CELLS), lambda i: (0, i, 0, 0))]
    in_specs += [block(r, wide) for r in (1, LOW, BAND, HIGH)]
    in_specs += [block(r, width) for r in (LOW, BAND, HIGH)]
    in_specs += [whole(weights.shape)]
    operands = [code, *states, *cots, weights]
    aliases = {}
    if earlier is not None:
        aliases = {len(operands): 4}
        in_specs.append(whole(weights.shape))
        operands.append(earlier)
    out_shape = [jax.ShapeDtypeStruct((1, r, cols, wide), BF16) for r in (1, LOW, BAND, HIGH)]
    out_shape.append(jax.ShapeDtypeStruct(weights.shape, F32))
    many = SLOTS * cols
    return pl.pallas_call(
        functools.partial(kernel, earlier is None),
        grid=(cols // STEP,),
        in_specs=in_specs,
        out_specs=[block(r, wide) for r in (1, LOW, BAND, HIGH)] + [whole(weights.shape)],
        out_shape=out_shape,
        scratch_shapes=[
            pltpu.VMEM((SLOTS * STEP, 3 * width), BF16),
            pltpu.VMEM((SLOTS * STEP, 3 * width), BF16),
        ],
        input_output_aliases=aliases,
        compiler_params=pltpu.CompilerParams(vmem_limit_bytes=48 * 1024 * 1024),
        cost_estimate=pl.CostEstimate(
            flops=6 * many * wide * 3 * width + 10 * many * 128 * width * 2,
            bytes_accessed=many * (4 * wide + 2 * width) + 8 * wide * 3 * width,
            transcendentals=many * 128 * 6,
        ),
    )(*operands)


def group_codes(group_ids):
    rows = group_ids.shape[-1]
    same = group_ids[:, :, :, None] == group_ids[:, :, None, :]
    at = jnp.arange(rows)
    before = jnp.sum(same & (at[None, :] < at[:, None]), axis=-1)
    after = jnp.sum(same & (at[None, :] > at[:, None]), axis=-1)
    start, end = at - before, at + after
    first, last = start // BAND, end // BAND
    border = last * BAND
    owner = jnp.where((first != last) & (border - start > end + 1 - border), first, last)
    return (group_ids + 8 * owner).astype(jnp.int32)


def slot_codes(codes, band):
    tables, cols, rows = codes.shape
    padded = jnp.pad(codes, ((0, 0), (0, 0), (LOW, HIGH)), constant_values=-8)
    near = lax.dynamic_slice_in_dim(padded, band * BAND, LOW + BAND + HIGH, axis=2)
    row = band * BAND - LOW + jnp.arange(LOW + BAND + HIGH)
    alive = (near >> 3) == band
    mark = (jnp.arange(cols) % SUB)[None, :, None] * 8 + (near & 7)
    query = jnp.where(alive, mark, -1)
    key = jnp.where(alive & (row != 0), mark, -2)

    def order(values, header):
        values = jnp.pad(values, ((0, 0), (0, 0), (1, 0)), constant_values=header)
        values = values.reshape(tables, cols // STEP, STEP // SUB, SUB, SLOTS)
        return values.transpose(0, 1, 2, 4, 3).reshape(tables, cols // STEP, STEP // SUB, CELLS)

    return jnp.concatenate((order(query, -1), order(key, -2)), axis=2).astype(jnp.int32)


def halo_body(cell_states, head_grads, group_ids, proj_weights):
    bands = lax.axis_size("band")
    band = lax.axis_index("band")
    tables = cell_states.shape[0]
    up = [(i, i + 1) for i in range(bands - 1)]
    down = [(i + 1, i) for i in range(bands - 1)]
    send = lambda a, pairs: lax.ppermute(a, "band", pairs)
    far = [(0, bands // 2)]
    near = [(0, 1), (bands // 2, bands // 2 + 1)]
    back = lambda pairs: [(b, a) for a, b in pairs]

    codes = lax.all_gather(group_codes(group_ids), "band", axis=1, tiled=True)
    codes = slot_codes(codes, band)
    weight_sum = None
    outputs = []
    for t in range(tables):
        states, cots = cell_states[t : t + 1], head_grads[t : t + 1]
        mine = states[:, :1]
        mine = jnp.where(band == bands // 2, send(mine, far), mine)
        header = jnp.where(band % 2 == 1, send(mine, near), mine)
        pieces = (
            header,
            send(states[:, BAND - LOW :], up),
            states,
            send(states[:, :HIGH], down),
        )
        cot_pieces = (send(cots[:, BAND - LOW :], up), cots, send(cots[:, :HIGH], down))
        out_h, out_l, out_o, out_u, weight_sum = attend(
            codes[t : t + 1], pieces, cot_pieces, proj_weights, weight_sum
        )
        from_high = send(out_l, down).astype(F32)
        from_low = send(out_u, up).astype(F32)
        head = out_h.astype(F32) + send(out_h, back(near)).astype(F32)
        head = head + send(head.astype(BF16), back(far)).astype(F32)
        head = jnp.where(band == 0, head, 0.0)
        whole = out_o.astype(F32)
        pad = lambda a, lo: jnp.pad(a, ((0, 0), (lo, BAND - lo - a.shape[1]), (0, 0), (0, 0)))
        whole = whole + pad(from_high, BAND - LOW) + pad(from_low, 0) + pad(head, 0)
        outputs.append(whole.astype(BF16))
    shared = lax.psum_scatter(weight_sum, "band", scatter_dimension=0, tiled=True)
    weight_grad = lax.psum_scatter(shared, "dp", scatter_dimension=1, tiled=True)
    return (jnp.concatenate(outputs, axis=0), weight_grad)


def normalize(states):
    widened = states.astype(jnp.float32)
    meansq = jnp.mean(widened * widened, axis=-1, keepdims=True)
    inverse = lax.rsqrt(meansq + EPSILON)
    scaled = widened * inverse
    return (scaled, inverse, scaled.astype(jnp.bfloat16))


def project(normed, weights):
    width = weights.shape[1] // 3
    flat = normed.reshape(-1, normed.shape[-1])
    mixed = jnp.dot(flat, weights, preferred_element_type=jnp.float32).astype(jnp.bfloat16)
    mixed = mixed.reshape(normed.shape[:-1] + (3 * width,))
    return (mixed[..., :width], mixed[..., width : 2 * width], mixed[..., 2 * width :])


def attend_back(query_rows, key_rows, value_rows, grad_rows, groups):
    shape = query_rows.shape
    split = shape[:-1] + (shape[-1] // HD, HD)
    query_five = query_rows.reshape(split)
    key_five = key_rows.reshape(split)
    value_five = value_rows.reshape(split)
    grad_five = grad_rows.reshape(split)
    scores = (
        jnp.einsum("bichd,bjchd->bchij", query_five, key_five, preferred_element_type=jnp.float32)
        * SCALE
    )
    header = lax.broadcasted_iota(jnp.int32, (shape[1], shape[1]), 1) == 0
    visible = (groups[:, :, :, None] == groups[:, :, None, :]) | header
    scores = jnp.where(visible[:, :, None], scores, -1e30)
    peak = jnp.max(scores, axis=-1, keepdims=True)
    expsc = jnp.exp(scores - peak)
    probs = expsc / jnp.sum(expsc, axis=-1, keepdims=True)
    probs_low = probs.astype(jnp.bfloat16)
    value_grad = jnp.einsum(
        "bchij,bichd->bjchd", probs_low, grad_five, preferred_element_type=jnp.float32
    ).astype(jnp.bfloat16)
    prob_grad = jnp.einsum(
        "bichd,bjchd->bchij", grad_five, value_five, preferred_element_type=jnp.float32
    )
    score_grad = probs * (prob_grad - jnp.sum(probs * prob_grad, axis=-1, keepdims=True))
    score_low = (score_grad * SCALE).astype(jnp.bfloat16)
    query_grad = jnp.einsum(
        "bchij,bjchd->bichd", score_low, key_five, preferred_element_type=jnp.float32
    ).astype(jnp.bfloat16)
    key_grad = jnp.einsum(
        "bchij,bichd->bjchd", score_low, query_five, preferred_element_type=jnp.float32
    ).astype(jnp.bfloat16)
    return (query_grad.reshape(shape), key_grad.reshape(shape), value_grad.reshape(shape))


def finish(scaled, inverse, normed, all_grads, weights):
    flat_norm = normed.reshape(-1, normed.shape[-1])
    flat_grad = all_grads.reshape(-1, all_grads.shape[-1])
    partial_w = lax.dot_general(
        flat_norm, flat_grad, (((0,), (0,)), ((), ())), preferred_element_type=jnp.float32
    )
    normed_grad = lax.dot_general(
        flat_grad, weights, (((1,), (1,)), ((), ())), preferred_element_type=jnp.float32
    )
    normed_grad = normed_grad.reshape(scaled.shape)
    coupling = jnp.mean(normed_grad * scaled, axis=-1, keepdims=True)
    state_grad = (inverse * (normed_grad - scaled * coupling)).astype(jnp.bfloat16)
    return (partial_w, state_grad)


def exchange_body(cell_states, head_grads, group_ids, proj_weights):
    scaled, inverse, normed = normalize(cell_states)
    query_rows, key_rows, value_rows = project(normed, proj_weights)
    query_cols, key_cols, value_cols, grad_cols = (
        lax.all_to_all(query_rows, "band", split_axis=2, concat_axis=1, tiled=True),
        lax.all_to_all(key_rows, "band", split_axis=2, concat_axis=1, tiled=True),
        lax.all_to_all(value_rows, "band", split_axis=2, concat_axis=1, tiled=True),
        lax.all_to_all(head_grads, "band", split_axis=2, concat_axis=1, tiled=True),
    )
    query_grad, key_grad, value_grad = attend_back(
        query_cols, key_cols, value_cols, grad_cols, group_ids
    )
    query_home, key_home, value_home = (
        lax.all_to_all(query_grad, "band", split_axis=1, concat_axis=2, tiled=True),
        lax.all_to_all(key_grad, "band", split_axis=1, concat_axis=2, tiled=True),
        lax.all_to_all(value_grad, "band", split_axis=1, concat_axis=2, tiled=True),
    )
    all_grads = jnp.concatenate((query_home, key_home, value_home), axis=-1)
    partial_w, input_grad = finish(scaled, inverse, normed, all_grads, proj_weights)
    shared = lax.psum_scatter(partial_w, "dp", scatter_dimension=1, tiled=True)
    weight_grad = lax.psum_scatter(shared, "band", scatter_dimension=0, tiled=True)
    return (input_grad, weight_grad)


def body(cell_states, head_grads, group_ids, proj_weights):
    halo = cell_states.shape[1] == BAND and lax.axis_size("band") == 4
    form = halo_body if halo else exchange_body
    return form(cell_states, head_grads, group_ids, proj_weights)


def solution(mesh):
    return jax.shard_map(
        body,
        mesh=mesh,
        in_specs=(
            P("dp", "band", None, None),
            P("dp", "band", None, None),
            P("dp", "band", None),
            P(),
        ),
        out_specs=(P("dp", "band", None, None), P("band", "dp")),
        check_vma=False,
    )
```

```python
import jax
import jax.numpy as jnp
from jax import lax
from jax.experimental import pallas as pl
from jax.experimental.pallas import tpu as pltpu
from jax.sharding import PartitionSpec as P

HD = 64
SCALE = 0.125
EPSILON = 1e-06
LOW = 4
HIGH = 3
BAND = 8
BANDS = 4
SHARES = 8
SLOTS = 1 + LOW + BAND + HIGH
SUB = 8
STEP = 16
CELLS = SLOTS * SUB
CHUNK = 64
DEEP = 1024
F32 = jnp.float32
BF16 = jnp.bfloat16
MESH = pl.DeviceIdType.MESH


def dot(a, b, ca, cb):
    return lax.dot_general(a, b, (((ca,), (cb,)), ((), ())), preferred_element_type=F32)


def kernel(
    code_in, x, g, w, out, wout,
    code, hx, lx, ux, lg, ug, from_high, from_low, from_head,
    normed_all, grads_all, mixed, acc, half_send, half_recv,
    x_send, x_recv, y_send, y_recv, z_send, z_recv, fin, fin_recv,
    code_ss, code_rs, halo_ss, halo_rs, head_ss, head_rs, back_ss, back_rs, top_ss, top_rs,
    half_ss, half_rs, x_ss, x_rs, y_ss, y_rs, z_ss, z_rs, fin_ss, fin_rs,
):
    tables, _, cols, wide = x.shape
    width = g.shape[-1]
    per_table = cols // CHUNK
    chunks = tables * per_table
    band, share = lax.axis_index("band"), lax.axis_index("dp")
    core, side = lax.rem(band, 2), band // 2
    y, z = lax.rem(share, 2), share // 2
    sibling, across = side * 2 + 1 - core, (1 - side) * 2 + core

    def copy(src, dst, ss, rs, **where):
        return pltpu.make_async_remote_copy(
            src_ref=src, dst_ref=dst, send_sem=ss, recv_sem=rs, device_id=where, device_id_type=MESH
        )

    barrier = pltpu.get_barrier_semaphore()
    for k in range(1, BANDS):
        pl.semaphore_signal(
            barrier, inc=1, device_id={"band": lax.rem(band + k, BANDS)}, device_id_type=MESH
        )
    pl.semaphore_signal(barrier, inc=1, device_id={"dp": z * 2 + 1 - y}, device_id_type=MESH)
    for k in range(1, SHARES // 2):
        other = lax.rem(z + k, SHARES // 2) * 2 + y
        pl.semaphore_signal(barrier, inc=1, device_id={"dp": other}, device_id_type=MESH)
    pl.semaphore_wait(barrier, BANDS + SHARES // 2 - 1)

    def place(c):
        return c // per_table, pl.ds(pl.multiple_of(lax.rem(c, per_table) * CHUNK, CHUNK), CHUNK)

    def code_copy(k):
        to = lax.rem(band + k, BANDS)
        return copy(code_in.at[to], code.at[band], code_ss.at[k - 1], code_rs.at[k - 1], band=to)

    def code_arrival(k):
        source = lax.rem(band + BANDS - k, BANDS)
        return copy(code_in.at[source], code.at[source], code_ss.at[k - 1], code_rs.at[k - 1], band=source)

    def head_copy(c, to):
        t, at = place(c)
        return copy(
            x.at[t, pl.ds(0, 1), at], hx.at[t, :, at], head_ss.at[to - 1, c], head_rs.at[c], band=to
        )

    def up_copies(c, to):
        t, at = place(c)
        rows = pl.ds(BAND - LOW, LOW)
        return (
            copy(x.at[t, rows, at], lx.at[t, :, at], halo_ss.at[0, c], halo_rs.at[0, c], band=to),
            copy(g.at[t, rows, at], lg.at[t, :, at], halo_ss.at[1, c], halo_rs.at[1, c], band=to),
        )

    def down_copies(c, to):
        t, at = place(c)
        rows = pl.ds(0, HIGH)
        return (
            copy(x.at[t, rows, at], ux.at[t, :, at], halo_ss.at[2, c], halo_rs.at[2, c], band=to),
            copy(g.at[t, rows, at], ug.at[t, :, at], halo_ss.at[3, c], halo_rs.at[3, c], band=to),
        )

    def back_low(c, to):
        t, at = place(c)
        return copy(lx.at[t, :, at], from_high.at[t, :, at], back_ss.at[0, c], back_rs.at[0, c], band=to)

    def back_high(c, to):
        t, at = place(c)
        return copy(ux.at[t, :, at], from_low.at[t, :, at], back_ss.at[1, c], back_rs.at[1, c], band=to)

    def back_head(c, source):
        t, at = place(c)
        return copy(
            hx.at[t, :, at], from_head.at[source - 1, t, :, at], top_ss.at[c], top_rs.at[source - 1, c],
            band=0,
        )

    has_low, has_high = band > 0, band < BANDS - 1

    for k in range(1, BANDS):
        code_copy(k).start()

    def send_chunk(c, carry):
        @pl.when(band == 0)
        def _():
            for to in range(1, BANDS):
                head_copy(c, to).start()

        @pl.when(has_high)
        def _():
            for one in up_copies(c, band + 1):
                one.start()

        @pl.when(has_low)
        def _():
            for one in down_copies(c, band - 1):
                one.start()

        return carry

    lax.fori_loop(0, chunks, send_chunk, 0)

    code[band] = code_in[band]

    @pl.when(band == 0)
    def _():
        hx[...] = x[:, 0:1]
        lx[...] = jnp.zeros_like(lx)
        lg[...] = jnp.zeros_like(lg)

    @pl.when(band == BANDS - 1)
    def _():
        ux[...] = jnp.zeros_like(ux)
        ug[...] = jnp.zeros_like(ug)

    for k in range(1, BANDS):
        code_arrival(k).wait_recv()

    lane = lax.broadcasted_iota(jnp.int32, (1, 128), 1)
    left = jnp.where(lane < HD, 1.0, 0.0).astype(BF16)
    right = jnp.where(lane < HD, 0.0, 1.0).astype(BF16)

    def split_heads(a):
        return jnp.concatenate((a * left, a * right), axis=0)

    def flat(parts):
        whole = jnp.concatenate(parts, axis=0).astype(F32)
        return jnp.concatenate(
            [whole[:, s : s + SUB].reshape(CELLS, whole.shape[-1]) for s in range(0, STEP, SUB)], axis=0
        )

    def step(t, at_step, many):
        at = pl.ds(pl.multiple_of(at_step * STEP, STEP), STEP)
        rows_all = pl.ds(pl.multiple_of(many * SLOTS * STEP, SLOTS * STEP), SLOTS * STEP)
        states = flat((hx[t, :, at], lx[t, :, at], x[t, :, at], ux[t, :, at]))
        inverse = lax.rsqrt(jnp.mean(states * states, axis=-1, keepdims=True) + EPSILON)
        scaled = states * inverse
        normed = scaled.astype(BF16)
        normed_all[rows_all] = normed
        mixed[...] = dot(normed, w[...], 1, 0).astype(BF16)
        cotangent = flat((jnp.zeros((1, STEP, width), BF16), lg[t, :, at], g[t, :, at], ug[t, :, at]))
        cotangent = cotangent.astype(BF16)
        marks = code[at_step // 2, t, lax.rem(at_step, 2)]
        biases = []
        for s in range(STEP // SUB):
            query_code = marks[s : s + 1]
            key_code = jnp.broadcast_to(marks[s + 2 : s + 3], (CELLS, CELLS)).T
            row = lax.broadcasted_iota(jnp.int32, (CELLS, CELLS), 0)
            visible = (key_code == query_code) | (row == (query_code >> 3))
            biases.append(jnp.where(visible, 0.0, -1e30).astype(F32))
        units = [(s, p) for s in range(STEP // SUB) for p in range(width // 128)]

        def part(kind, s, p):
            start = kind * width + 128 * p
            return mixed[s * CELLS : (s + 1) * CELLS, start : start + 128]

        scale = jnp.asarray(SCALE, BF16)
        grad = [cotangent[s * CELLS : (s + 1) * CELLS, 128 * p : 128 * p + 128] for s, p in units]
        query = [part(0, s, p) * scale for s, p in units]
        scores = [
            dot(split_heads(part(1, s, p)), q, 1, 1).reshape(2, CELLS, CELLS)
            for (s, p), q in zip(units, query)
        ]
        prob_grad = [
            dot(split_heads(part(2, s, p)), d, 1, 1).reshape(2, CELLS, CELLS)
            for (s, p), d in zip(units, grad)
        ]
        all_grads = {}
        for n, (s, p) in enumerate(units):
            masked = scores[n] + biases[s][None]
            peak = jnp.maximum(jnp.max(masked, axis=1, keepdims=True), -1e29)
            expsc = jnp.exp(masked - peak)
            total = jnp.maximum(jnp.sum(expsc, axis=1, keepdims=True), 1.0)
            probs = expsc * (1.0 / total)
            delta = jnp.sum(probs * prob_grad[n], axis=1, keepdims=True)
            score_low = (probs * (prob_grad[n] - delta)).astype(BF16)
            probs_low = probs.astype(BF16)
            value_grad = dot(
                jnp.concatenate((probs_low[0], probs_low[1]), axis=1), split_heads(grad[n]), 1, 0
            )
            key_grad = dot(
                jnp.concatenate((score_low[0], score_low[1]), axis=1), split_heads(query[n]), 1, 0
            )
            query_grad = dot(
                score_low.reshape(2 * CELLS, CELLS), split_heads(part(1, s, p) * scale), 0, 0
            )
            all_grads[s, 0, p] = query_grad.astype(BF16)
            all_grads[s, 1, p] = key_grad.astype(BF16)
            all_grads[s, 2, p] = value_grad.astype(BF16)
        joined = jnp.concatenate(
            [
                jnp.concatenate([all_grads[s, k, p] for k in range(3) for p in range(width // 128)], axis=1)
                for s in range(STEP // SUB)
            ],
            axis=0,
        )
        grads_all[rows_all] = joined
        normed_grad = dot(joined, w[...], 1, 1)
        coupling = jnp.mean(normed_grad * scaled, axis=-1, keepdims=True)
        result = inverse * (normed_grad - scaled * coupling)
        pieces = [result[s * CELLS : (s + 1) * CELLS].reshape(SLOTS, SUB, wide) for s in range(STEP // SUB)]
        result = jnp.concatenate(pieces, axis=1).astype(BF16)
        hx[t, :, at] = result[:1]
        lx[t, :, at] = result[1 : 1 + LOW]
        out[t, :, at] = result[1 + LOW : 1 + LOW + BAND]
        ux[t, :, at] = result[1 + LOW + BAND :]

    steps = CHUNK // STEP

    def work_chunk(c, carry):
        @pl.when(band > 0)
        def _():
            head_copy(c, 1).wait_recv()

        @pl.when(has_low)
        def _():
            for one in up_copies(c, 0):
                one.wait_recv()

        @pl.when(has_high)
        def _():
            for one in down_copies(c, 0):
                one.wait_recv()

        def one_step(i, carry):
            step(c // per_table, lax.rem(c, per_table) * steps + i, c * steps + i)
            return carry

        lax.fori_loop(0, steps, one_step, 0)

        @pl.when(has_low)
        def _():
            back_low(c, band - 1).start()

        @pl.when(has_high)
        def _():
            back_high(c, band + 1).start()

        for source in range(1, BANDS):

            @pl.when(band == source)
            def _():
                back_head(c, source).start()

        return carry

    lax.fori_loop(0, chunks, work_chunk, 0)

    total_rows = grads_all.shape[0]
    block = 3 * width // SHARES
    rows_half = SHARES // 2 * block
    mine = pl.ds(pl.multiple_of(core * rows_half, 16), rows_half)
    theirs = pl.ds(pl.multiple_of((1 - core) * rows_half, 16), rows_half)

    def product(n, which):
        lanes = pl.ds(pl.multiple_of(which * (wide // 2), 128), wide // 2)
        acc[n] = jnp.zeros(acc.shape[1:], F32)

        def deep(i, carry):
            at = pl.ds(pl.multiple_of(i * DEEP, DEEP), DEEP)
            acc[n] += dot(grads_all[at, :], normed_all[at, lanes], 0, 0)
            return carry

        lax.fori_loop(0, total_rows // DEEP, deep, 0)
        half_send[n] = acc[n, theirs, :].astype(BF16)

    def half_copy(n):
        return copy(half_send.at[n], half_recv.at[n], half_ss.at[n], half_rs.at[n], band=sibling)

    product(0, 1 - side)
    half_copy(0).start()
    product(1, side)
    half_copy(1).start()
    half_copy(0).wait_recv()
    x_send[...] = (acc[0, mine, :] + half_recv[0].astype(F32)).astype(BF16)
    x_copy = copy(x_send, x_recv, x_ss, x_rs, band=across)
    x_copy.start()

    def merge_chunk(c, carry):
        t, at = place(c)

        @pl.when(has_high)
        def _():
            back_low(c, 0).wait_recv()
            rows = pl.ds(BAND - LOW, LOW)
            out[t, rows, at] = (out[t, rows, at].astype(F32) + from_high[t, :, at].astype(F32)).astype(BF16)

        @pl.when(has_low)
        def _():
            back_high(c, 0).wait_recv()
            rows = pl.ds(0, HIGH)
            out[t, rows, at] = (out[t, rows, at].astype(F32) + from_low[t, :, at].astype(F32)).astype(BF16)

        @pl.when(band == 0)
        def _():
            top = out[t, 0:1, at].astype(F32) + hx[t, :, at].astype(F32)
            for source in range(1, BANDS):
                back_head(c, source).wait_recv()
                top = top + from_head[source - 1, t, :, at].astype(F32)
            out[t, 0:1, at] = top.astype(BF16)

        return carry

    lax.fori_loop(0, chunks, merge_chunk, 0)

    half_copy(1).wait_recv()
    x_copy.wait_recv()
    kept = acc[1, mine, :] + half_recv[1].astype(F32) + x_recv[...].astype(F32)
    kept = kept.reshape(SHARES // 4, 2, block, wide // 2)
    acc_y = jnp.where(y == 0, kept[:, 0], kept[:, 1])
    y_send[...] = jnp.where(y == 0, kept[:, 1], kept[:, 0]).astype(BF16)
    y_copy = copy(y_send, y_recv, y_ss, y_rs, dp=z * 2 + 1 - y)
    y_copy.start()
    y_copy.wait_recv()
    acc_z = acc_y + y_recv[...].astype(F32)
    z_send[...] = acc_z.astype(BF16)

    def z_copy(j, source):
        return copy(z_send.at[j], z_recv.at[source], z_ss.at[j], z_rs.at[source], dp=(2 * core + j) * 2 + y)

    zs = SHARES // 2
    for j in range(2):
        for source in range(zs):

            @pl.when((z == source) & (2 * core + j != z))
            def _():
                z_copy(j, source).start()

    fin_copy = copy(fin, fin_recv, fin_ss, fin_rs, band=sibling)
    holder = z // 2 == core

    def emit(full):
        half = wide // 4
        wout[...] = jnp.where(core == 0, full[:, :half], full[:, half:])

    @pl.when(holder)
    def _():
        fin[...] = jnp.where(lax.rem(z, 2) == 0, acc_z[0], acc_z[1])
        for source in range(zs):

            @pl.when(z != source)
            def _():
                z_copy(0, source).wait_recv()
                fin[...] += z_recv[source].astype(F32)

        fin_copy.start()
        emit(fin[...])
        fin_copy.wait_send()

    @pl.when(jnp.logical_not(holder))
    def _():
        fin_copy.wait_recv()
        emit(fin_recv[...])

    for k in range(1, BANDS):
        code_copy(k).wait_send()

    def drain(c, carry):
        @pl.when(band == 0)
        def _():
            for to in range(1, BANDS):
                head_copy(c, to).wait_send()

        @pl.when(has_high)
        def _():
            for one in up_copies(c, band + 1):
                one.wait_send()
            back_high(c, band + 1).wait_send()

        @pl.when(has_low)
        def _():
            for one in down_copies(c, band - 1):
                one.wait_send()
            back_low(c, band - 1).wait_send()
            back_head(c, 1).wait_send()

        return carry

    lax.fori_loop(0, chunks, drain, 0)
    half_copy(0).wait_send()
    half_copy(1).wait_send()
    x_copy.wait_send()
    y_copy.wait_send()
    for j in range(2):

        @pl.when(2 * core + j != z)
        def _():
            z_copy(j, 0).wait_send()


def group_codes(group_ids):
    rows = group_ids.shape[-1]
    same = group_ids[:, :, :, None] == group_ids[:, :, None, :]
    at = jnp.arange(rows)
    before = jnp.sum(same & (at[None, :] < at[:, None]), axis=-1)
    after = jnp.sum(same & (at[None, :] > at[:, None]), axis=-1)
    start, end = at - before, at + after
    first, last = start // BAND, end // BAND
    border = last * BAND
    owner = jnp.where((first != last) & (border - start > end + 1 - border), first, last)
    return (group_ids + 8 * owner).astype(jnp.int32)


def slot_codes(codes, band):
    tables, cols, rows = codes.shape
    padded = jnp.pad(codes, ((0, 0), (0, 0), (LOW, HIGH)), constant_values=-8)
    near = padded[:, :, band * BAND : band * BAND + LOW + BAND + HIGH]
    row = band * BAND - LOW + jnp.arange(LOW + BAND + HIGH)
    alive = (near >> 3) == band
    mark = (jnp.arange(cols) % SUB)[None, :, None] * 8 + (near & 7)
    query = jnp.where(alive, mark, -1)
    key = jnp.where(alive & (row != 0), mark, -2)

    def order(values, header):
        values = jnp.pad(values, ((0, 0), (0, 0), (1, 0)), constant_values=header)
        values = values.reshape(tables, cols // STEP, STEP // SUB, SUB, SLOTS)
        return values.transpose(0, 1, 2, 4, 3).reshape(tables, cols // STEP, STEP // SUB, CELLS)

    return jnp.concatenate((order(query, -1), order(key, -2)), axis=2).astype(jnp.int32)


def halo_body(cell_states, head_grads, group_ids, proj_weights):
    tables, _, cols, wide = cell_states.shape
    width = head_grads.shape[-1]
    codes = group_codes(group_ids)
    codes = jnp.stack([slot_codes(codes, b) for b in range(BANDS)])
    chunks = tables * cols // CHUNK
    many = SLOTS * tables * cols
    block = 3 * width // SHARES
    rows_half, lanes = 3 * width // 2, wide // 2
    halo = lambda rows, features: pltpu.VMEM((tables, rows, cols, features), BF16)
    sems = lambda *shape: pltpu.SemaphoreType.DMA(shape)
    pair = lambda *shape: [sems(*shape), sems(*shape)]
    one = pltpu.SemaphoreType.DMA
    vmem = pl.BlockSpec(memory_space=pltpu.VMEM)
    input_grad, turned = pl.pallas_call(
        kernel,
        in_specs=[vmem] * 4,
        out_specs=[vmem] * 2,
        out_shape=[
            jax.ShapeDtypeStruct(cell_states.shape, BF16),
            jax.ShapeDtypeStruct((block, wide // BANDS), F32),
        ],
        scratch_shapes=[
            pltpu.VMEM(codes.shape, jnp.int32),
            halo(1, wide), halo(LOW, wide), halo(HIGH, wide), halo(LOW, width), halo(HIGH, width),
            halo(LOW, wide), halo(HIGH, wide),
            pltpu.VMEM((BANDS - 1, tables, 1, cols, wide), BF16),
            pltpu.VMEM((many, wide), BF16),
            pltpu.VMEM((many, 3 * width), BF16),
            pltpu.VMEM((SLOTS * STEP, 3 * width), BF16),
            pltpu.VMEM((2, 3 * width, lanes), F32),
            pltpu.VMEM((2, rows_half, lanes), BF16),
            pltpu.VMEM((2, rows_half, lanes), BF16),
            pltpu.VMEM((rows_half, lanes), BF16),
            pltpu.VMEM((rows_half, lanes), BF16),
            pltpu.VMEM((2, block, lanes), BF16),
            pltpu.VMEM((2, block, lanes), BF16),
            pltpu.VMEM((2, block, lanes), BF16),
            pltpu.VMEM((SHARES // 2, block, lanes), BF16),
            pltpu.VMEM((block, lanes), F32),
            pltpu.VMEM((block, lanes), F32),
            *pair(BANDS - 1),
            *pair(4, chunks),
            sems(BANDS - 1, chunks), sems(chunks),
            *pair(2, chunks),
            sems(chunks), sems(BANDS - 1, chunks),
            *pair(2),
            one, one,
            one, one,
            sems(2), sems(SHARES // 2),
            one, one,
        ],
        compiler_params=pltpu.CompilerParams(
            collective_id=0, has_side_effects=True, vmem_limit_bytes=60 * 1024 * 1024
        ),
        cost_estimate=pl.CostEstimate(
            flops=6 * many * wide * 3 * width + 10 * many * 128 * width * 2,
            bytes_accessed=many * (2 * wide + width),
            transcendentals=many * 128 * 6,
        ),
    )(codes, cell_states, head_grads, proj_weights)
    return (input_grad, turned.T)


def normalize(states):
    widened = states.astype(jnp.float32)
    meansq = jnp.mean(widened * widened, axis=-1, keepdims=True)
    inverse = lax.rsqrt(meansq + EPSILON)
    scaled = widened * inverse
    return (scaled, inverse, scaled.astype(jnp.bfloat16))


def project(normed, weights):
    width = weights.shape[1] // 3
    flat = normed.reshape(-1, normed.shape[-1])
    mixed = jnp.dot(flat, weights, preferred_element_type=jnp.float32).astype(jnp.bfloat16)
    mixed = mixed.reshape(normed.shape[:-1] + (3 * width,))
    return (mixed[..., :width], mixed[..., width : 2 * width], mixed[..., 2 * width :])


def attend_back(query_rows, key_rows, value_rows, grad_rows, groups):
    shape = query_rows.shape
    split = shape[:-1] + (shape[-1] // HD, HD)
    query_five = query_rows.reshape(split)
    key_five = key_rows.reshape(split)
    value_five = value_rows.reshape(split)
    grad_five = grad_rows.reshape(split)
    scores = (
        jnp.einsum("bichd,bjchd->bchij", query_five, key_five, preferred_element_type=jnp.float32)
        * SCALE
    )
    header = lax.broadcasted_iota(jnp.int32, (shape[1], shape[1]), 1) == 0
    visible = (groups[:, :, :, None] == groups[:, :, None, :]) | header
    scores = jnp.where(visible[:, :, None], scores, -1e30)
    peak = jnp.max(scores, axis=-1, keepdims=True)
    expsc = jnp.exp(scores - peak)
    probs = expsc / jnp.sum(expsc, axis=-1, keepdims=True)
    probs_low = probs.astype(jnp.bfloat16)
    value_grad = jnp.einsum(
        "bchij,bichd->bjchd", probs_low, grad_five, preferred_element_type=jnp.float32
    ).astype(jnp.bfloat16)
    prob_grad = jnp.einsum(
        "bichd,bjchd->bchij", grad_five, value_five, preferred_element_type=jnp.float32
    )
    score_grad = probs * (prob_grad - jnp.sum(probs * prob_grad, axis=-1, keepdims=True))
    score_low = (score_grad * SCALE).astype(jnp.bfloat16)
    query_grad = jnp.einsum(
        "bchij,bjchd->bichd", score_low, key_five, preferred_element_type=jnp.float32
    ).astype(jnp.bfloat16)
    key_grad = jnp.einsum(
        "bchij,bichd->bjchd", score_low, query_five, preferred_element_type=jnp.float32
    ).astype(jnp.bfloat16)
    return (query_grad.reshape(shape), key_grad.reshape(shape), value_grad.reshape(shape))


def finish(scaled, inverse, normed, all_grads, weights):
    flat_norm = normed.reshape(-1, normed.shape[-1])
    flat_grad = all_grads.reshape(-1, all_grads.shape[-1])
    partial_w = lax.dot_general(
        flat_norm, flat_grad, (((0,), (0,)), ((), ())), preferred_element_type=jnp.float32
    )
    normed_grad = lax.dot_general(
        flat_grad, weights, (((1,), (1,)), ((), ())), preferred_element_type=jnp.float32
    )
    normed_grad = normed_grad.reshape(scaled.shape)
    coupling = jnp.mean(normed_grad * scaled, axis=-1, keepdims=True)
    state_grad = (inverse * (normed_grad - scaled * coupling)).astype(jnp.bfloat16)
    return (partial_w, state_grad)


def exchange_body(cell_states, head_grads, group_ids, proj_weights):
    scaled, inverse, normed = normalize(cell_states)
    query_rows, key_rows, value_rows = project(normed, proj_weights)
    query_cols, key_cols, value_cols, grad_cols = (
        lax.all_to_all(query_rows, "band", split_axis=2, concat_axis=1, tiled=True),
        lax.all_to_all(key_rows, "band", split_axis=2, concat_axis=1, tiled=True),
        lax.all_to_all(value_rows, "band", split_axis=2, concat_axis=1, tiled=True),
        lax.all_to_all(head_grads, "band", split_axis=2, concat_axis=1, tiled=True),
    )
    query_grad, key_grad, value_grad = attend_back(
        query_cols, key_cols, value_cols, grad_cols, group_ids
    )
    query_home, key_home, value_home = (
        lax.all_to_all(query_grad, "band", split_axis=1, concat_axis=2, tiled=True),
        lax.all_to_all(key_grad, "band", split_axis=1, concat_axis=2, tiled=True),
        lax.all_to_all(value_grad, "band", split_axis=1, concat_axis=2, tiled=True),
    )
    all_grads = jnp.concatenate((query_home, key_home, value_home), axis=-1)
    partial_w, input_grad = finish(scaled, inverse, normed, all_grads, proj_weights)
    shared = lax.psum_scatter(partial_w, "dp", scatter_dimension=1, tiled=True)
    weight_grad = lax.psum_scatter(shared, "band", scatter_dimension=0, tiled=True)
    return (input_grad, weight_grad)


def body(cell_states, head_grads, group_ids, proj_weights):
    halo = cell_states.shape[1] == BAND
    halo = halo and lax.axis_size("band") == BANDS and lax.axis_size("dp") == SHARES
    form = halo_body if halo else exchange_body
    return form(cell_states, head_grads, group_ids, proj_weights)


def solution(mesh):
    return jax.shard_map(
        body,
        mesh=mesh,
        in_specs=(
            P("dp", "band", None, None),
            P("dp", "band", None, None),
            P("dp", "band", None),
            P(),
        ),
        out_specs=(P("dp", "band", None, None), P("band", "dp")),
        check_vma=False,
    )
```

```python
import jax
import jax.numpy as jnp
from jax import lax
from jax.experimental import pallas as pl
from jax.experimental.pallas import tpu as pltpu
from jax.sharding import PartitionSpec as P

HD = 64
SCALE = 0.125
EPSILON = 1e-06
LOW = 4
HIGH = 3
BAND = 8
BANDS = 4
SHARES = 8
SLOTS = 1 + LOW + BAND + HIGH
SUB = 8
STEP = 32
CELLS = SLOTS * SUB
CHUNK = 32
AHEAD = 2
DEEP = 1024
F32 = jnp.float32
BF16 = jnp.bfloat16
MESH = pl.DeviceIdType.MESH


def dot(a, b, ca, cb):
    return lax.dot_general(a, b, (((ca,), (cb,)), ((), ())), preferred_element_type=F32)


def kernel(
    code_in, x, g, w, out, wout,
    code, hx, lx, ux, lg, ug, from_high, from_low, from_head,
    normed_all, grads_all, mixed, acc, half_send, half_recv,
    x_send, x_recv, y_send, y_recv, z_send, z_recv, fin, fin_recv,
    code_ss, code_rs, halo_ss, halo_rs, head_ss, head_rs, back_ss, back_rs, top_ss, top_rs,
    half_ss, half_rs, x_ss, x_rs, y_ss, y_rs, z_ss, z_rs, fin_ss, fin_rs,
):
    tables, _, cols, wide = x.shape
    width = g.shape[-1]
    per_table = cols // CHUNK
    chunks = tables * per_table
    per_band = cols // BANDS // STEP
    band, share = lax.axis_index("band"), lax.axis_index("dp")
    core, side = lax.rem(band, 2), band // 2
    y, z = lax.rem(share, 2), share // 2
    sibling, across = side * 2 + 1 - core, (1 - side) * 2 + core

    def copy(src, dst, ss, rs, **where):
        return pltpu.make_async_remote_copy(
            src_ref=src, dst_ref=dst, send_sem=ss, recv_sem=rs, device_id=where, device_id_type=MESH
        )

    barrier = pltpu.get_barrier_semaphore()
    for k in range(1, BANDS):
        pl.semaphore_signal(
            barrier, inc=1, device_id={"band": lax.rem(band + k, BANDS)}, device_id_type=MESH
        )
    pl.semaphore_signal(barrier, inc=1, device_id={"dp": z * 2 + 1 - y}, device_id_type=MESH)
    for k in range(1, SHARES // 2):
        other = lax.rem(z + k, SHARES // 2) * 2 + y
        pl.semaphore_signal(barrier, inc=1, device_id={"dp": other}, device_id_type=MESH)
    pl.semaphore_wait(barrier, BANDS + SHARES // 2 - 1)

    def place(c):
        return c // per_table, pl.ds(pl.multiple_of(lax.rem(c, per_table) * CHUNK, CHUNK), CHUNK)

    def code_copy(k):
        to = lax.rem(band + k, BANDS)
        return copy(code_in.at[to], code.at[band], code_ss.at[k - 1], code_rs.at[k - 1], band=to)

    def code_arrival(k):
        source = lax.rem(band + BANDS - k, BANDS)
        return copy(code_in.at[source], code.at[source], code_ss.at[k - 1], code_rs.at[k - 1], band=source)

    def head_copy(c, to):
        t, at = place(c)
        return copy(
            x.at[t, pl.ds(0, 1), at], hx.at[t, :, at], head_ss.at[to - 1, c], head_rs.at[c], band=to
        )

    def up_copies(c, to):
        t, at = place(c)
        rows = pl.ds(BAND - LOW, LOW)
        return (
            copy(x.at[t, rows, at], lx.at[t, :, at], halo_ss.at[0, c], halo_rs.at[0, c], band=to),
            copy(g.at[t, rows, at], lg.at[t, :, at], halo_ss.at[1, c], halo_rs.at[1, c], band=to),
        )

    def down_copies(c, to):
        t, at = place(c)
        rows = pl.ds(0, HIGH)
        return (
            copy(x.at[t, rows, at], ux.at[t, :, at], halo_ss.at[2, c], halo_rs.at[2, c], band=to),
            copy(g.at[t, rows, at], ug.at[t, :, at], halo_ss.at[3, c], halo_rs.at[3, c], band=to),
        )

    def back_low(c, to):
        t, at = place(c)
        return copy(lx.at[t, :, at], from_high.at[t, :, at], back_ss.at[0, c], back_rs.at[0, c], band=to)

    def back_high(c, to):
        t, at = place(c)
        return copy(ux.at[t, :, at], from_low.at[t, :, at], back_ss.at[1, c], back_rs.at[1, c], band=to)

    def back_head(c, source):
        t, at = place(c)
        return copy(
            hx.at[t, :, at], from_head.at[source - 1, t, :, at], top_ss.at[c], top_rs.at[source - 1, c],
            band=0,
        )

    has_low, has_high = band > 0, band < BANDS - 1

    for k in range(1, BANDS):
        code_copy(k).start()

    def send_chunk(c, carry):
        @pl.when(band == 0)
        def _():
            for to in range(1, BANDS):
                head_copy(c, to).start()

        @pl.when(has_high)
        def _():
            for one in up_copies(c, band + 1):
                one.start()

        @pl.when(has_low)
        def _():
            for one in down_copies(c, band - 1):
                one.start()

        return carry

    lax.fori_loop(0, AHEAD, send_chunk, 0)

    code[band] = code_in[band]

    @pl.when(band == 0)
    def _():
        hx[...] = x[:, 0:1]
        lx[...] = jnp.zeros_like(lx)
        lg[...] = jnp.zeros_like(lg)

    @pl.when(band == BANDS - 1)
    def _():
        ux[...] = jnp.zeros_like(ux)
        ug[...] = jnp.zeros_like(ug)

    for k in range(1, BANDS):
        code_arrival(k).wait_recv()

    lane = lax.broadcasted_iota(jnp.int32, (1, 128), 1)
    left = jnp.where(lane < HD, 1.0, 0.0).astype(BF16)
    right = jnp.where(lane < HD, 0.0, 1.0).astype(BF16)

    def split_heads(a):
        return jnp.concatenate((a * left, a * right), axis=0)

    def flat(parts):
        whole = jnp.concatenate(parts, axis=0).astype(F32)
        return jnp.concatenate(
            [whole[:, s : s + SUB].reshape(CELLS, whole.shape[-1]) for s in range(0, STEP, SUB)], axis=0
        )

    def step(t, at_step, many):
        at = pl.ds(pl.multiple_of(at_step * STEP, STEP), STEP)
        rows_all = pl.ds(pl.multiple_of(many * SLOTS * STEP, SLOTS * STEP), SLOTS * STEP)
        states = flat((hx[t, :, at], lx[t, :, at], x[t, :, at], ux[t, :, at]))
        inverse = lax.rsqrt(jnp.mean(states * states, axis=-1, keepdims=True) + EPSILON)
        scaled = states * inverse
        normed = scaled.astype(BF16)
        normed_all[rows_all] = normed
        mixed[...] = dot(normed, w[...], 1, 0).astype(BF16)
        cotangent = flat((jnp.zeros((1, STEP, width), BF16), lg[t, :, at], g[t, :, at], ug[t, :, at]))
        cotangent = cotangent.astype(BF16)
        marks = code[at_step // per_band, t, lax.rem(at_step, per_band)]
        biases = []
        for s in range(STEP // SUB):
            query_code = marks[s : s + 1]
            key_code = jnp.broadcast_to(marks[STEP // SUB + s : STEP // SUB + s + 1], (CELLS, CELLS)).T
            row = lax.broadcasted_iota(jnp.int32, (CELLS, CELLS), 0)
            visible = (key_code == query_code) | (row == (query_code >> 3))
            biases.append(jnp.where(visible, 0.0, -1e30).astype(F32))
        units = [(s, p) for s in range(STEP // SUB) for p in range(width // 128)]

        def part(kind, s, p):
            start = kind * width + 128 * p
            return mixed[s * CELLS : (s + 1) * CELLS, start : start + 128]

        scale = jnp.asarray(SCALE, BF16)
        grad = [cotangent[s * CELLS : (s + 1) * CELLS, 128 * p : 128 * p + 128] for s, p in units]
        query = [part(0, s, p) * scale for s, p in units]
        scores = [
            dot(split_heads(part(1, s, p)), q, 1, 1).reshape(2, CELLS, CELLS)
            for (s, p), q in zip(units, query)
        ]
        prob_grad = [
            dot(split_heads(part(2, s, p)), d, 1, 1).reshape(2, CELLS, CELLS)
            for (s, p), d in zip(units, grad)
        ]
        all_grads = {}
        for n, (s, p) in enumerate(units):
            masked = scores[n] + biases[s][None]
            peak = jnp.maximum(jnp.max(masked, axis=1, keepdims=True), -1e29)
            expsc = jnp.exp(masked - peak)
            total = jnp.maximum(jnp.sum(expsc, axis=1, keepdims=True), 1.0)
            probs = expsc * (1.0 / total)
            delta = jnp.sum(probs * prob_grad[n], axis=1, keepdims=True)
            score_low = (probs * (prob_grad[n] - delta)).astype(BF16)
            probs_low = probs.astype(BF16)
            value_grad = dot(
                jnp.concatenate((probs_low[0], probs_low[1]), axis=1), split_heads(grad[n]), 1, 0
            )
            key_grad = dot(
                jnp.concatenate((score_low[0], score_low[1]), axis=1), split_heads(query[n]), 1, 0
            )
            query_grad = dot(
                score_low.reshape(2 * CELLS, CELLS), split_heads(part(1, s, p) * scale), 0, 0
            )
            all_grads[s, 0, p] = query_grad.astype(BF16)
            all_grads[s, 1, p] = key_grad.astype(BF16)
            all_grads[s, 2, p] = value_grad.astype(BF16)
        joined = jnp.concatenate(
            [
                jnp.concatenate([all_grads[s, k, p] for k in range(3) for p in range(width // 128)], axis=1)
                for s in range(STEP // SUB)
            ],
            axis=0,
        )
        grads_all[rows_all] = joined
        normed_grad = dot(joined, w[...], 1, 1)
        coupling = jnp.mean(normed_grad * scaled, axis=-1, keepdims=True)
        result = inverse * (normed_grad - scaled * coupling)
        pieces = [result[s * CELLS : (s + 1) * CELLS].reshape(SLOTS, SUB, wide) for s in range(STEP // SUB)]
        result = jnp.concatenate(pieces, axis=1).astype(BF16)
        hx[t, :, at] = result[:1]
        lx[t, :, at] = result[1 : 1 + LOW]
        out[t, :, at] = result[1 + LOW : 1 + LOW + BAND]
        ux[t, :, at] = result[1 + LOW + BAND :]

    steps = CHUNK // STEP

    def work_chunk(c, carry):
        @pl.when(band > 0)
        def _():
            head_copy(c, 1).wait_recv()

        @pl.when(has_low)
        def _():
            for one in up_copies(c, 0):
                one.wait_recv()

        @pl.when(has_high)
        def _():
            for one in down_copies(c, 0):
                one.wait_recv()

        @pl.when(c + AHEAD < chunks)
        def _():
            send_chunk(c + AHEAD, 0)

        def one_step(i, carry):
            step(c // per_table, lax.rem(c, per_table) * steps + i, c * steps + i)
            return carry

        lax.fori_loop(0, steps, one_step, 0)

        @pl.when(has_low)
        def _():
            back_low(c, band - 1).start()

        @pl.when(has_high)
        def _():
            back_high(c, band + 1).start()

        for source in range(1, BANDS):

            @pl.when(band == source)
            def _():
                back_head(c, source).start()

        return carry

    lax.fori_loop(0, chunks, work_chunk, 0)

    total_rows = grads_all.shape[0]
    block = 3 * width // SHARES
    rows_half = SHARES // 2 * block
    mine = pl.ds(pl.multiple_of(core * rows_half, 16), rows_half)
    theirs = pl.ds(pl.multiple_of((1 - core) * rows_half, 16), rows_half)

    def product(n, which, begin, end):
        lanes = pl.ds(pl.multiple_of(which * (wide // 2), 128), wide // 2)

        def deep(i, carry):
            at = pl.ds(pl.multiple_of(i * DEEP, DEEP), DEEP)
            acc[n] += dot(grads_all[at, :], normed_all[at, lanes], 0, 0)
            return carry

        lax.fori_loop(begin, end, deep, 0)

    def half_copy(n):
        return copy(half_send.at[n], half_recv.at[n], half_ss.at[n], half_rs.at[n], band=sibling)

    def x_copy(j):
        return copy(x_send.at[j], x_recv.at[j], x_ss.at[j], x_rs.at[j], band=across)

    def piece(j):
        return pl.ds(pl.multiple_of(core * rows_half + j * (2 * block), 16), 2 * block)

    deeps = total_rows // DEEP
    acc[...] = jnp.zeros_like(acc)
    product(0, 1 - side, 0, deeps)
    half_send[0] = acc[0, theirs, :].astype(BF16)
    half_copy(0).start()
    product(1, side, 0, 1)
    half_copy(0).wait_recv()
    for j in range(2):
        partner = half_recv[0, 2 * block * j : 2 * block * (j + 1)].astype(F32)
        x_send[j] = (acc[0, piece(j), :] + partner).astype(BF16)
        x_copy(j).start()
    product(1, side, 1, deeps)
    half_send[1] = acc[1, theirs, :].astype(BF16)
    half_copy(1).start()

    def merge_chunk(c, carry):
        t, at = place(c)

        @pl.when(has_high)
        def _():
            back_low(c, 0).wait_recv()
            rows = pl.ds(BAND - LOW, LOW)
            out[t, rows, at] = (out[t, rows, at].astype(F32) + from_high[t, :, at].astype(F32)).astype(BF16)

        @pl.when(has_low)
        def _():
            back_high(c, 0).wait_recv()
            rows = pl.ds(0, HIGH)
            out[t, rows, at] = (out[t, rows, at].astype(F32) + from_low[t, :, at].astype(F32)).astype(BF16)

        @pl.when(band == 0)
        def _():
            top = out[t, 0:1, at].astype(F32) + hx[t, :, at].astype(F32)
            for source in range(1, BANDS):
                back_head(c, source).wait_recv()
                top = top + from_head[source - 1, t, :, at].astype(F32)
            out[t, 0:1, at] = top.astype(BF16)

        return carry

    lax.fori_loop(0, chunks, merge_chunk, 0)

    def y_copy(j):
        return copy(y_send.at[j], y_recv.at[j], y_ss.at[j], y_rs.at[j], dp=z * 2 + 1 - y)

    half_copy(1).wait_recv()
    kept_y = []
    for j in range(2):
        x_copy(j).wait_recv()
        kept = acc[1, piece(j), :] + half_recv[1, 2 * block * j : 2 * block * (j + 1)].astype(F32)
        kept = (kept + x_recv[j].astype(F32)).reshape(2, block, wide // 2)
        kept_y.append(jnp.where(y == 0, kept[0], kept[1]))
        y_send[j] = jnp.where(y == 0, kept[1], kept[0]).astype(BF16)
        y_copy(j).start()

    def z_copy(j, source):
        return copy(z_send.at[j], z_recv.at[source], z_ss.at[j], z_rs.at[source], dp=(2 * core + j) * 2 + y)

    zs = SHARES // 2
    acc_z = []
    for j in range(2):
        y_copy(j).wait_recv()
        acc_z.append(kept_y[j] + y_recv[j].astype(F32))
        z_send[j] = acc_z[j].astype(BF16)
        for source in range(zs):

            @pl.when((z == source) & (2 * core + j != z))
            def _():
                z_copy(j, source).start()

    fin_copy = copy(fin, fin_recv, fin_ss, fin_rs, band=sibling)
    holder = z // 2 == core

    def emit(full):
        half = wide // 4
        wout[...] = jnp.where(core == 0, full[:, :half], full[:, half:])

    @pl.when(holder)
    def _():
        fin[...] = jnp.where(lax.rem(z, 2) == 0, acc_z[0], acc_z[1])
        for source in range(zs):

            @pl.when(z != source)
            def _():
                z_copy(0, source).wait_recv()
                fin[...] += z_recv[source].astype(F32)

        fin_copy.start()
        emit(fin[...])
        fin_copy.wait_send()

    @pl.when(jnp.logical_not(holder))
    def _():
        fin_copy.wait_recv()
        emit(fin_recv[...])

    for k in range(1, BANDS):
        code_copy(k).wait_send()

    def drain(c, carry):
        @pl.when(band == 0)
        def _():
            for to in range(1, BANDS):
                head_copy(c, to).wait_send()

        @pl.when(has_high)
        def _():
            for one in up_copies(c, band + 1):
                one.wait_send()
            back_high(c, band + 1).wait_send()

        @pl.when(has_low)
        def _():
            for one in down_copies(c, band - 1):
                one.wait_send()
            back_low(c, band - 1).wait_send()
            back_head(c, 1).wait_send()

        return carry

    lax.fori_loop(0, chunks, drain, 0)
    half_copy(0).wait_send()
    half_copy(1).wait_send()
    for j in range(2):
        x_copy(j).wait_send()
        y_copy(j).wait_send()

        @pl.when(2 * core + j != z)
        def _():
            z_copy(j, 0).wait_send()


def group_codes(group_ids):
    bands = group_ids.reshape(group_ids.shape[:2] + (BANDS, BAND))
    first = bands[..., :1]
    following = jnp.pad(first[:, :, 1:], ((0, 0), (0, 0), (0, 1), (0, 0)), constant_values=-1)
    tail = bands == following
    head = bands == first
    below = jnp.sum(tail, axis=-1, keepdims=True)
    above = jnp.sum(head, axis=-1, keepdims=True)
    above_next = jnp.pad(above[:, :, 1:], ((0, 0), (0, 0), (0, 1), (0, 0)))
    below_last = jnp.pad(below[:, :, :-1], ((0, 0), (0, 0), (1, 0), (0, 0)))
    goes_up = tail & (below <= above_next)
    goes_down = head & (below_last > above)
    owner = jnp.arange(BANDS)[:, None] + goes_up.astype(jnp.int32) - goes_down.astype(jnp.int32)
    return (bands + 8 * owner).astype(jnp.int32).reshape(group_ids.shape)


def slot_codes(codes, band):
    tables, cols, rows = codes.shape
    padded = jnp.pad(codes, ((0, 0), (0, 0), (LOW, HIGH)), constant_values=-8)
    near = padded[:, :, band * BAND : band * BAND + LOW + BAND + HIGH]
    row = band * BAND - LOW + jnp.arange(LOW + BAND + HIGH)
    alive = (near >> 3) == band
    mark = (jnp.arange(cols) % SUB)[None, :, None] * 8 + (near & 7)
    query = jnp.where(alive, mark, -1)
    key = jnp.where(alive & (row != 0), mark, -2)

    def order(values, header):
        values = jnp.pad(values, ((0, 0), (0, 0), (1, 0)), constant_values=header)
        values = values.reshape(tables, cols // STEP, STEP // SUB, SUB, SLOTS)
        return values.transpose(0, 1, 2, 4, 3).reshape(tables, cols // STEP, STEP // SUB, CELLS)

    return jnp.concatenate((order(query, -1), order(key, -2)), axis=2).astype(jnp.int32)


def halo_body(cell_states, head_grads, group_ids, proj_weights):
    tables, _, cols, wide = cell_states.shape
    width = head_grads.shape[-1]
    codes = group_codes(group_ids)
    codes = jnp.stack([slot_codes(codes, b) for b in range(BANDS)])
    chunks = tables * cols // CHUNK
    many = SLOTS * tables * cols
    block = 3 * width // SHARES
    rows_half, lanes = 3 * width // 2, wide // 2
    halo = lambda rows, features: pltpu.VMEM((tables, rows, cols, features), BF16)
    sems = lambda *shape: pltpu.SemaphoreType.DMA(shape)
    pair = lambda *shape: [sems(*shape), sems(*shape)]
    one = pltpu.SemaphoreType.DMA
    vmem = pl.BlockSpec(memory_space=pltpu.VMEM)
    input_grad, turned = pl.pallas_call(
        kernel,
        in_specs=[vmem] * 4,
        out_specs=[vmem] * 2,
        out_shape=[
            jax.ShapeDtypeStruct(cell_states.shape, BF16),
            jax.ShapeDtypeStruct((block, wide // BANDS), F32),
        ],
        scratch_shapes=[
            pltpu.VMEM(codes.shape, jnp.int32),
            halo(1, wide), halo(LOW, wide), halo(HIGH, wide), halo(LOW, width), halo(HIGH, width),
            halo(LOW, wide), halo(HIGH, wide),
            pltpu.VMEM((BANDS - 1, tables, 1, cols, wide), BF16),
            pltpu.VMEM((many, wide), BF16),
            pltpu.VMEM((many, 3 * width), BF16),
            pltpu.VMEM((SLOTS * STEP, 3 * width), BF16),
            pltpu.VMEM((2, 3 * width, lanes), F32),
            pltpu.VMEM((2, rows_half, lanes), BF16),
            pltpu.VMEM((2, rows_half, lanes), BF16),
            pltpu.VMEM((2, 2 * block, lanes), BF16),
            pltpu.VMEM((2, 2 * block, lanes), BF16),
            pltpu.VMEM((2, block, lanes), BF16),
            pltpu.VMEM((2, block, lanes), BF16),
            pltpu.VMEM((2, block, lanes), BF16),
            pltpu.VMEM((SHARES // 2, block, lanes), BF16),
            pltpu.VMEM((block, lanes), F32),
            pltpu.VMEM((block, lanes), F32),
            *pair(BANDS - 1),
            *pair(4, chunks),
            sems(BANDS - 1, chunks), sems(chunks),
            *pair(2, chunks),
            sems(chunks), sems(BANDS - 1, chunks),
            *pair(2),
            *pair(2),
            *pair(2),
            sems(2), sems(SHARES // 2),
            one, one,
        ],
        compiler_params=pltpu.CompilerParams(
            collective_id=0, has_side_effects=True, vmem_limit_bytes=60 * 1024 * 1024
        ),
        cost_estimate=pl.CostEstimate(
            flops=6 * many * wide * 3 * width + 10 * many * 128 * width * 2,
            bytes_accessed=many * (2 * wide + width),
            transcendentals=many * 128 * 6,
        ),
    )(codes, cell_states, head_grads, proj_weights)
    return (input_grad, turned.T)


def normalize(states):
    widened = states.astype(jnp.float32)
    meansq = jnp.mean(widened * widened, axis=-1, keepdims=True)
    inverse = lax.rsqrt(meansq + EPSILON)
    scaled = widened * inverse
    return (scaled, inverse, scaled.astype(jnp.bfloat16))


def project(normed, weights):
    width = weights.shape[1] // 3
    flat = normed.reshape(-1, normed.shape[-1])
    mixed = jnp.dot(flat, weights, preferred_element_type=jnp.float32).astype(jnp.bfloat16)
    mixed = mixed.reshape(normed.shape[:-1] + (3 * width,))
    return (mixed[..., :width], mixed[..., width : 2 * width], mixed[..., 2 * width :])


def attend_back(query_rows, key_rows, value_rows, grad_rows, groups):
    shape = query_rows.shape
    split = shape[:-1] + (shape[-1] // HD, HD)
    query_five = query_rows.reshape(split)
    key_five = key_rows.reshape(split)
    value_five = value_rows.reshape(split)
    grad_five = grad_rows.reshape(split)
    scores = (
        jnp.einsum("bichd,bjchd->bchij", query_five, key_five, preferred_element_type=jnp.float32)
        * SCALE
    )
    header = lax.broadcasted_iota(jnp.int32, (shape[1], shape[1]), 1) == 0
    visible = (groups[:, :, :, None] == groups[:, :, None, :]) | header
    scores = jnp.where(visible[:, :, None], scores, -1e30)
    peak = jnp.max(scores, axis=-1, keepdims=True)
    expsc = jnp.exp(scores - peak)
    probs = expsc / jnp.sum(expsc, axis=-1, keepdims=True)
    probs_low = probs.astype(jnp.bfloat16)
    value_grad = jnp.einsum(
        "bchij,bichd->bjchd", probs_low, grad_five, preferred_element_type=jnp.float32
    ).astype(jnp.bfloat16)
    prob_grad = jnp.einsum(
        "bichd,bjchd->bchij", grad_five, value_five, preferred_element_type=jnp.float32
    )
    score_grad = probs * (prob_grad - jnp.sum(probs * prob_grad, axis=-1, keepdims=True))
    score_low = (score_grad * SCALE).astype(jnp.bfloat16)
    query_grad = jnp.einsum(
        "bchij,bjchd->bichd", score_low, key_five, preferred_element_type=jnp.float32
    ).astype(jnp.bfloat16)
    key_grad = jnp.einsum(
        "bchij,bichd->bjchd", score_low, query_five, preferred_element_type=jnp.float32
    ).astype(jnp.bfloat16)
    return (query_grad.reshape(shape), key_grad.reshape(shape), value_grad.reshape(shape))


def finish(scaled, inverse, normed, all_grads, weights):
    flat_norm = normed.reshape(-1, normed.shape[-1])
    flat_grad = all_grads.reshape(-1, all_grads.shape[-1])
    partial_w = lax.dot_general(
        flat_norm, flat_grad, (((0,), (0,)), ((), ())), preferred_element_type=jnp.float32
    )
    normed_grad = lax.dot_general(
        flat_grad, weights, (((1,), (1,)), ((), ())), preferred_element_type=jnp.float32
    )
    normed_grad = normed_grad.reshape(scaled.shape)
    coupling = jnp.mean(normed_grad * scaled, axis=-1, keepdims=True)
    state_grad = (inverse * (normed_grad - scaled * coupling)).astype(jnp.bfloat16)
    return (partial_w, state_grad)


def exchange_body(cell_states, head_grads, group_ids, proj_weights):
    scaled, inverse, normed = normalize(cell_states)
    query_rows, key_rows, value_rows = project(normed, proj_weights)
    query_cols, key_cols, value_cols, grad_cols = (
        lax.all_to_all(query_rows, "band", split_axis=2, concat_axis=1, tiled=True),
        lax.all_to_all(key_rows, "band", split_axis=2, concat_axis=1, tiled=True),
        lax.all_to_all(value_rows, "band", split_axis=2, concat_axis=1, tiled=True),
        lax.all_to_all(head_grads, "band", split_axis=2, concat_axis=1, tiled=True),
    )
    query_grad, key_grad, value_grad = attend_back(
        query_cols, key_cols, value_cols, grad_cols, group_ids
    )
    query_home, key_home, value_home = (
        lax.all_to_all(query_grad, "band", split_axis=1, concat_axis=2, tiled=True),
        lax.all_to_all(key_grad, "band", split_axis=1, concat_axis=2, tiled=True),
        lax.all_to_all(value_grad, "band", split_axis=1, concat_axis=2, tiled=True),
    )
    all_grads = jnp.concatenate((query_home, key_home, value_home), axis=-1)
    partial_w, input_grad = finish(scaled, inverse, normed, all_grads, proj_weights)
    shared = lax.psum_scatter(partial_w, "dp", scatter_dimension=1, tiled=True)
    weight_grad = lax.psum_scatter(shared, "band", scatter_dimension=0, tiled=True)
    return (input_grad, weight_grad)


def body(cell_states, head_grads, group_ids, proj_weights):
    halo = cell_states.shape[1] == BAND
    halo = halo and lax.axis_size("band") == BANDS and lax.axis_size("dp") == SHARES
    form = halo_body if halo else exchange_body
    return form(cell_states, head_grads, group_ids, proj_weights)


def solution(mesh):
    return jax.shard_map(
        body,
        mesh=mesh,
        in_specs=(
            P("dp", "band", None, None),
            P("dp", "band", None, None),
            P("dp", "band", None),
            P(),
        ),
        out_specs=(P("dp", "band", None, None), P("band", "dp")),
        check_vma=False,
    )
```

```python
import jax
import jax.numpy as jnp
from jax import lax
from jax.experimental import pallas as pl
from jax.experimental.pallas import tpu as pltpu
from jax.sharding import PartitionSpec as P

HD = 64
SCALE = 0.125
EPSILON = 1e-06
LOW = 4
HIGH = 3
BAND = 8
BANDS = 4
SHARES = 8
SLOTS = 1 + LOW + BAND + HIGH
SUB = 8
STEP = 32
CELLS = SLOTS * SUB
CHUNK = STEP
AHEAD = 2
LATE = 4
DEEP = 1024
F32 = jnp.float32
BF16 = jnp.bfloat16
MESH = pl.DeviceIdType.MESH


def dot(a, b, ca, cb):
    return lax.dot_general(a, b, (((ca,), (cb,)), ((), ())), preferred_element_type=F32)


def kernel(
    code_in, x_in, g_in, w_in, out, wout, x, g, w,
    code, hx, lx, ux, lg, ug, from_high, from_low, from_head,
    normed_all, grads_t, grads_late, mixed, acc, half_send, half_recv,
    x_send, x_recv, kept, y_send, y_recv, z_send, z_recv, fin, fin_recv,
    code_ss, code_rs, halo_ss, halo_rs, head_ss, head_rs, back_ss, back_rs, top_ss, top_rs,
    load_x, load_g, load_w, load_h,
    half_ss, half_rs, x_ss, x_rs, y_ss, y_rs, z_ss, z_rs, fin_ss, fin_rs,
):
    tables, _, cols, wide = x_in.shape
    width = g_in.shape[-1]
    per_table = cols // CHUNK
    chunks = tables * per_table
    per_band = cols // BANDS // STEP
    band, share = lax.axis_index("band"), lax.axis_index("dp")
    core, side = lax.rem(band, 2), band // 2
    y, z = lax.rem(share, 2), share // 2
    sibling, across = side * 2 + 1 - core, (1 - side) * 2 + core

    def copy(src, dst, ss, rs, **where):
        return pltpu.make_async_remote_copy(
            src_ref=src, dst_ref=dst, send_sem=ss, recv_sem=rs, device_id=where, device_id_type=MESH
        )

    def loads(t):
        return (
            pltpu.make_async_copy(x_in.at[t], x.at[t], load_x.at[t]),
            pltpu.make_async_copy(g_in.at[t], g.at[t], load_g.at[t]),
        )

    weight_load = pltpu.make_async_copy(w_in, w, load_w)
    weight_load.start()
    for t in range(tables):
        for one in loads(t):
            one.start()

    barrier = pltpu.get_barrier_semaphore()
    for k in range(1, BANDS):
        pl.semaphore_signal(
            barrier, inc=1, device_id={"band": lax.rem(band + k, BANDS)}, device_id_type=MESH
        )
    pl.semaphore_signal(barrier, inc=1, device_id={"dp": z * 2 + 1 - y}, device_id_type=MESH)
    for k in range(1, SHARES // 2):
        other = lax.rem(z + k, SHARES // 2) * 2 + y
        pl.semaphore_signal(barrier, inc=1, device_id={"dp": other}, device_id_type=MESH)
    pl.semaphore_wait(barrier, BANDS + SHARES // 2 - 1)

    def place(c):
        return c // per_table, pl.ds(pl.multiple_of(lax.rem(c, per_table) * CHUNK, CHUNK), CHUNK)

    def code_copy(k):
        to = lax.rem(band + k, BANDS)
        return copy(code_in.at[to], code.at[band], code_ss.at[k - 1], code_rs.at[k - 1], band=to)

    def code_arrival(k):
        source = lax.rem(band + BANDS - k, BANDS)
        return copy(code_in.at[source], code.at[source], code_ss.at[k - 1], code_rs.at[k - 1], band=source)

    def head_copy(c, to):
        t, at = place(c)
        return copy(
            x_in.at[t, pl.ds(0, 1), at], hx.at[t, :, at], head_ss.at[to - 1, c], head_rs.at[c], band=to
        )

    def up_copies(c, to):
        t, at = place(c)
        rows = pl.ds(BAND - LOW, LOW)
        return (
            copy(x_in.at[t, rows, at], lx.at[t, :, at], halo_ss.at[0, c], halo_rs.at[0, c], band=to),
            copy(g_in.at[t, rows, at], lg.at[t, :, at], halo_ss.at[1, c], halo_rs.at[1, c], band=to),
        )

    def down_copies(c, to):
        t, at = place(c)
        rows = pl.ds(0, HIGH)
        return (
            copy(x_in.at[t, rows, at], ux.at[t, :, at], halo_ss.at[2, c], halo_rs.at[2, c], band=to),
            copy(g_in.at[t, rows, at], ug.at[t, :, at], halo_ss.at[3, c], halo_rs.at[3, c], band=to),
        )

    def back_low(c, to):
        t, at = place(c)
        return copy(lx.at[t, :, at], from_high.at[t, :, at], back_ss.at[0, c], back_rs.at[0, c], band=to)

    def back_high(c, to):
        t, at = place(c)
        return copy(ux.at[t, :, at], from_low.at[t, :, at], back_ss.at[1, c], back_rs.at[1, c], band=to)

    def back_head(c, source):
        t, at = place(c)
        return copy(
            hx.at[t, :, at], from_head.at[source - 1, t, :, at], top_ss.at[c], top_rs.at[source - 1, c],
            band=0,
        )

    has_low, has_high = band > 0, band < BANDS - 1

    for k in range(1, BANDS):
        code_copy(k).start()

    def send_chunk(c, carry):
        @pl.when(band == 0)
        def _():
            for to in range(1, BANDS):
                head_copy(c, to).start()

        @pl.when(has_high)
        def _():
            for one in up_copies(c, band + 1):
                one.start()

        @pl.when(has_low)
        def _():
            for one in down_copies(c, band - 1):
                one.start()

        return carry

    lax.fori_loop(0, AHEAD, send_chunk, 0)

    code[band] = code_in[band]

    @pl.when(band == 0)
    def _():
        for t in range(tables):
            own = pltpu.make_async_copy(x_in.at[t, pl.ds(0, 1)], hx.at[t], load_h)
            own.start()
            own.wait()

        lx[...] = jnp.zeros_like(lx)
        lg[...] = jnp.zeros_like(lg)

    @pl.when(band == BANDS - 1)
    def _():
        ux[...] = jnp.zeros_like(ux)
        ug[...] = jnp.zeros_like(ug)

    for k in range(1, BANDS):
        code_arrival(k).wait_recv()

    weight_load.wait()
    lane = lax.broadcasted_iota(jnp.int32, (1, 128), 1)
    left = jnp.where(lane < HD, 1.0, 0.0).astype(BF16)
    right = jnp.where(lane < HD, 0.0, 1.0).astype(BF16)

    def split_heads(a):
        return jnp.concatenate((a * left, a * right), axis=0)

    def flat(parts):
        whole = jnp.concatenate(parts, axis=0).astype(F32)
        return jnp.concatenate(
            [whole[:, s : s + SUB].reshape(CELLS, whole.shape[-1]) for s in range(0, STEP, SUB)], axis=0
        )

    def norms(t, at):
        states = flat((hx[t, :, at], lx[t, :, at], x[t, :, at], ux[t, :, at]))
        inverse = lax.rsqrt(jnp.mean(states * states, axis=-1, keepdims=True) + EPSILON)
        return states * inverse, inverse

    def cells(c):
        return pl.ds(pl.multiple_of(c * SLOTS * STEP, SLOTS * STEP), SLOTS * STEP)

    def grads_of(c):
        t, at = place(c)
        at_step = lax.rem(c, per_table)
        scaled, inverse = norms(t, at)
        rows_all = cells(c)
        normed = scaled.astype(BF16)
        normed_all[rows_all] = normed
        mixed[...] = dot(normed, w[...], 1, 0).astype(BF16)
        cotangent = flat((jnp.zeros((1, STEP, width), BF16), lg[t, :, at], g[t, :, at], ug[t, :, at]))
        cotangent = cotangent.astype(BF16)
        marks = code[at_step // per_band, t, lax.rem(at_step, per_band)]
        biases = []
        for s in range(STEP // SUB):
            query_code = marks[s : s + 1]
            key_code = jnp.broadcast_to(marks[STEP // SUB + s : STEP // SUB + s + 1], (CELLS, CELLS)).T
            row = lax.broadcasted_iota(jnp.int32, (CELLS, CELLS), 0)
            visible = (key_code == query_code) | (row == (query_code >> 3))
            biases.append(jnp.where(visible, 0.0, -1e30).astype(F32))
        units = [(s, p) for s in range(STEP // SUB) for p in range(width // 128)]

        def part(kind, s, p):
            start = kind * width + 128 * p
            return mixed[s * CELLS : (s + 1) * CELLS, start : start + 128]

        scale = jnp.asarray(SCALE, BF16)
        grad = [cotangent[s * CELLS : (s + 1) * CELLS, 128 * p : 128 * p + 128] for s, p in units]
        query = [part(0, s, p) * scale for s, p in units]
        scores = [
            dot(split_heads(part(1, s, p)), q, 1, 1).reshape(2, CELLS, CELLS)
            for (s, p), q in zip(units, query)
        ]
        prob_grad = [
            dot(split_heads(part(2, s, p)), d, 1, 1).reshape(2, CELLS, CELLS)
            for (s, p), d in zip(units, grad)
        ]
        all_grads = {}
        for n, (s, p) in enumerate(units):
            masked = scores[n] + biases[s][None]
            peak = jnp.maximum(jnp.max(masked, axis=1, keepdims=True), -1e29)
            expsc = jnp.exp(masked - peak)
            total = jnp.maximum(jnp.sum(expsc, axis=1, keepdims=True), 1.0)
            probs = expsc * (1.0 / total)
            delta = jnp.sum(probs * prob_grad[n], axis=1, keepdims=True)
            score_low = (probs * (prob_grad[n] - delta)).astype(BF16)
            probs_low = probs.astype(BF16)
            value_grad = dot(
                jnp.concatenate((probs_low[0], probs_low[1]), axis=1), split_heads(grad[n]), 1, 0
            )
            key_grad = dot(
                jnp.concatenate((score_low[0], score_low[1]), axis=1), split_heads(query[n]), 1, 0
            )
            query_grad = dot(
                score_low.reshape(2 * CELLS, CELLS), split_heads(part(1, s, p) * scale), 0, 0
            )
            all_grads[s, 0, p] = query_grad.astype(BF16)
            all_grads[s, 1, p] = key_grad.astype(BF16)
            all_grads[s, 2, p] = value_grad.astype(BF16)
        joined = jnp.concatenate(
            [
                jnp.concatenate([all_grads[s, k, p] for k in range(3) for p in range(width // 128)], axis=1)
                for s in range(STEP // SUB)
            ],
            axis=0,
        )
        turned = joined.T
        grads_t[:, rows_all] = turned
        return scaled, inverse, joined

    def finish(c, scaled, inverse, joined):
        t, at = place(c)
        normed_grad = dot(joined, w[...], 1, 1)
        coupling = jnp.mean(normed_grad * scaled, axis=-1, keepdims=True)
        result = inverse * (normed_grad - scaled * coupling)
        pieces = [result[s * CELLS : (s + 1) * CELLS].reshape(SLOTS, SUB, wide) for s in range(STEP // SUB)]
        result = jnp.concatenate(pieces, axis=1).astype(BF16)
        hx[t, :, at] = result[:1]
        lx[t, :, at] = result[1 : 1 + LOW]
        out[t, :, at] = result[1 + LOW : 1 + LOW + BAND]
        ux[t, :, at] = result[1 + LOW + BAND :]

        @pl.when(has_low)
        def _():
            back_low(c, band - 1).start()

        @pl.when(has_high)
        def _():
            back_high(c, band + 1).start()

        for source in range(1, BANDS):

            @pl.when(band == source)
            def _():
                back_head(c, source).start()

    def arrive(c):
        @pl.when(lax.rem(c, per_table) == 0)
        def _():
            for one in loads(c // per_table):
                one.wait()

        @pl.when(band > 0)
        def _():
            head_copy(c, 1).wait_recv()

        @pl.when(has_low)
        def _():
            for one in up_copies(c, 0):
                one.wait_recv()

        @pl.when(has_high)
        def _():
            for one in down_copies(c, 0):
                one.wait_recv()

        @pl.when(c + AHEAD < chunks)
        def _():
            send_chunk(c + AHEAD, 0)

    early = chunks - LATE

    def work_early(c, carry):
        arrive(c)
        finish(c, *grads_of(c))
        return carry

    def work_late(c, carry):
        arrive(c)
        grads_late[cells(c - early)] = grads_of(c)[2]
        return carry

    def end_late(c, carry):
        t, at = place(c)
        scaled, inverse = norms(t, at)
        finish(c, scaled, inverse, grads_late[cells(c - early)])
        return carry

    def late(n):
        lax.fori_loop(early + n, early + n + 1, end_late, 0)

    lax.fori_loop(0, early, work_early, 0)
    lax.fori_loop(early, chunks, work_late, 0)

    total_rows = normed_all.shape[0]
    block = 3 * width // SHARES
    rows_half = SHARES // 2 * block
    mine = pl.ds(pl.multiple_of(core * rows_half, 16), rows_half)
    theirs = pl.ds(pl.multiple_of((1 - core) * rows_half, 16), rows_half)

    def product(n, which, begin, end):
        lanes = pl.ds(pl.multiple_of(which * (wide // 2), 128), wide // 2)

        def deep(i, carry):
            at = pl.ds(pl.multiple_of(i * DEEP, DEEP), DEEP)
            acc[n] += dot(grads_t[:, at], normed_all[at, lanes], 1, 0)
            return carry

        lax.fori_loop(begin, end, deep, 0)

    def half_copy(n):
        return copy(half_send.at[n], half_recv.at[n], half_ss.at[n], half_rs.at[n], band=sibling)

    def x_copy(j):
        return copy(x_send.at[j], x_recv.at[j], x_ss.at[j], x_rs.at[j], band=across)

    def piece(j):
        return pl.ds(pl.multiple_of(core * rows_half + j * (2 * block), 16), 2 * block)

    deeps = total_rows // DEEP
    acc[...] = jnp.zeros_like(acc)
    product(0, 1 - side, 0, deeps)
    half_send[0] = acc[0, theirs, :].astype(BF16)
    half_copy(0).start()
    product(1, side, 0, 1)
    half_copy(0).wait_recv()
    for j in range(2):
        partner = half_recv[0, 2 * block * j : 2 * block * (j + 1)].astype(F32)
        x_send[j] = (acc[0, piece(j), :] + partner).astype(BF16)
        x_copy(j).start()
    product(1, side, 1, deeps)
    half_send[1] = acc[1, theirs, :].astype(BF16)
    half_copy(1).start()

    def y_copy(j):
        return copy(y_send.at[j], y_recv.at[j], y_ss.at[j], y_rs.at[j], dp=z * 2 + 1 - y)

    late(0)
    half_copy(1).wait_recv()
    for j in range(2):
        x_copy(j).wait_recv()
        whole = acc[1, piece(j), :] + half_recv[1, 2 * block * j : 2 * block * (j + 1)].astype(F32)
        whole = (whole + x_recv[j].astype(F32)).reshape(2, block, wide // 2)
        kept[j] = jnp.where(y == 0, whole[0], whole[1])
        y_send[j] = jnp.where(y == 0, whole[1], whole[0]).astype(BF16)
        y_copy(j).start()

    def z_copy(j, source):
        return copy(z_send.at[j], z_recv.at[source], z_ss.at[j], z_rs.at[source], dp=(2 * core + j) * 2 + y)

    zs = SHARES // 2
    late(1)
    for j in range(2):
        y_copy(j).wait_recv()
        kept[j] += y_recv[j].astype(F32)
        z_send[j] = kept[j].astype(BF16)
        for source in range(zs):

            @pl.when((z == source) & (2 * core + j != z))
            def _():
                z_copy(j, source).start()

    fin_copy = copy(fin, fin_recv, fin_ss, fin_rs, band=sibling)
    holder = z // 2 == core

    def emit(full):
        half = wide // 4
        wout[...] = jnp.where(core == 0, full[:, :half], full[:, half:])

    late(2)

    @pl.when(holder)
    def _():
        fin[...] = jnp.where(lax.rem(z, 2) == 0, kept[0], kept[1])
        for source in range(zs):

            @pl.when(z != source)
            def _():
                z_copy(0, source).wait_recv()
                fin[...] += z_recv[source].astype(F32)

        fin_copy.start()
        emit(fin[...])

    late(3)

    def merge_chunk(c, carry):
        t, at = place(c)

        @pl.when(has_high)
        def _():
            back_low(c, 0).wait_recv()
            rows = pl.ds(BAND - LOW, LOW)
            out[t, rows, at] = (out[t, rows, at].astype(F32) + from_high[t, :, at].astype(F32)).astype(BF16)

        @pl.when(has_low)
        def _():
            back_high(c, 0).wait_recv()
            rows = pl.ds(0, HIGH)
            out[t, rows, at] = (out[t, rows, at].astype(F32) + from_low[t, :, at].astype(F32)).astype(BF16)

        @pl.when(band == 0)
        def _():
            top = out[t, 0:1, at].astype(F32) + hx[t, :, at].astype(F32)
            for source in range(1, BANDS):
                back_head(c, source).wait_recv()
                top = top + from_head[source - 1, t, :, at].astype(F32)
            out[t, 0:1, at] = top.astype(BF16)

        return carry

    lax.fori_loop(0, chunks, merge_chunk, 0)

    @pl.when(holder)
    def _():
        fin_copy.wait_send()

    @pl.when(jnp.logical_not(holder))
    def _():
        fin_copy.wait_recv()
        emit(fin_recv[...])

    for k in range(1, BANDS):
        code_copy(k).wait_send()

    def drain(c, carry):
        @pl.when(band == 0)
        def _():
            for to in range(1, BANDS):
                head_copy(c, to).wait_send()

        @pl.when(has_high)
        def _():
            for one in up_copies(c, band + 1):
                one.wait_send()
            back_high(c, band + 1).wait_send()

        @pl.when(has_low)
        def _():
            for one in down_copies(c, band - 1):
                one.wait_send()
            back_low(c, band - 1).wait_send()
            back_head(c, 1).wait_send()

        return carry

    lax.fori_loop(0, chunks, drain, 0)
    half_copy(0).wait_send()
    half_copy(1).wait_send()
    for j in range(2):
        x_copy(j).wait_send()
        y_copy(j).wait_send()

        @pl.when(2 * core + j != z)
        def _():
            z_copy(j, 0).wait_send()


def group_codes(group_ids):
    bands = group_ids.reshape(group_ids.shape[:2] + (BANDS, BAND))
    first = bands[..., :1]
    following = jnp.pad(first[:, :, 1:], ((0, 0), (0, 0), (0, 1), (0, 0)), constant_values=-1)
    tail = bands == following
    head = bands == first
    below = jnp.sum(tail, axis=-1, keepdims=True)
    above = jnp.sum(head, axis=-1, keepdims=True)
    above_next = jnp.pad(above[:, :, 1:], ((0, 0), (0, 0), (0, 1), (0, 0)))
    below_last = jnp.pad(below[:, :, :-1], ((0, 0), (0, 0), (1, 0), (0, 0)))
    goes_up = tail & (below <= above_next)
    goes_down = head & (below_last > above)
    owner = jnp.arange(BANDS)[:, None] + goes_up.astype(jnp.int32) - goes_down.astype(jnp.int32)
    return (bands + 8 * owner).astype(jnp.int32).reshape(group_ids.shape)


def slot_codes(codes, band):
    tables, cols, rows = codes.shape
    padded = jnp.pad(codes, ((0, 0), (0, 0), (LOW, HIGH)), constant_values=-8)
    near = padded[:, :, band * BAND : band * BAND + LOW + BAND + HIGH]
    row = band * BAND - LOW + jnp.arange(LOW + BAND + HIGH)
    alive = (near >> 3) == band
    mark = (jnp.arange(cols) % SUB)[None, :, None] * 8 + (near & 7)
    query = jnp.where(alive, mark, -1)
    key = jnp.where(alive & (row != 0), mark, -2)

    def order(values, header):
        values = jnp.pad(values, ((0, 0), (0, 0), (1, 0)), constant_values=header)
        values = values.reshape(tables, cols // STEP, STEP // SUB, SUB, SLOTS)
        return values.transpose(0, 1, 2, 4, 3).reshape(tables, cols // STEP, STEP // SUB, CELLS)

    return jnp.concatenate((order(query, -1), order(key, -2)), axis=2).astype(jnp.int32)


def halo_body(cell_states, head_grads, group_ids, proj_weights):
    tables, _, cols, wide = cell_states.shape
    width = head_grads.shape[-1]
    codes = group_codes(group_ids)
    codes = jnp.stack([slot_codes(codes, b) for b in range(BANDS)])
    chunks = tables * cols // CHUNK
    many = SLOTS * tables * cols
    block = 3 * width // SHARES
    rows_half, lanes = 3 * width // 2, wide // 2
    halo = lambda rows, features: pltpu.VMEM((tables, rows, cols, features), BF16)
    sems = lambda *shape: pltpu.SemaphoreType.DMA(shape)
    pair = lambda *shape: [sems(*shape), sems(*shape)]
    one = pltpu.SemaphoreType.DMA
    vmem = pl.BlockSpec(memory_space=pltpu.VMEM)
    input_grad, turned = pl.pallas_call(
        kernel,
        in_specs=[vmem] + [pl.BlockSpec(memory_space=pl.ANY)] * 3,
        out_specs=[vmem] * 2,
        out_shape=[
            jax.ShapeDtypeStruct(cell_states.shape, BF16),
            jax.ShapeDtypeStruct((block, wide // BANDS), F32),
        ],
        scratch_shapes=[
            pltpu.VMEM(cell_states.shape, BF16),
            pltpu.VMEM(head_grads.shape, BF16),
            pltpu.VMEM(proj_weights.shape, BF16),
            pltpu.VMEM(codes.shape, jnp.int32),
            halo(1, wide), halo(LOW, wide), halo(HIGH, wide), halo(LOW, width), halo(HIGH, width),
            halo(LOW, wide), halo(HIGH, wide),
            pltpu.VMEM((BANDS - 1, tables, 1, cols, wide), BF16),
            pltpu.VMEM((many, wide), BF16),
            pltpu.VMEM((3 * width, many), BF16),
            pltpu.VMEM((LATE * SLOTS * STEP, 3 * width), BF16),
            pltpu.VMEM((SLOTS * STEP, 3 * width), BF16),
            pltpu.VMEM((2, 3 * width, lanes), F32),
            pltpu.VMEM((2, rows_half, lanes), BF16),
            pltpu.VMEM((2, rows_half, lanes), BF16),
            pltpu.VMEM((2, 2 * block, lanes), BF16),
            pltpu.VMEM((2, 2 * block, lanes), BF16),
            pltpu.VMEM((2, block, lanes), F32),
            pltpu.VMEM((2, block, lanes), BF16),
            pltpu.VMEM((2, block, lanes), BF16),
            pltpu.VMEM((2, block, lanes), BF16),
            pltpu.VMEM((SHARES // 2, block, lanes), BF16),
            pltpu.VMEM((block, lanes), F32),
            pltpu.VMEM((block, lanes), F32),
            *pair(BANDS - 1),
            *pair(4, chunks),
            sems(BANDS - 1, chunks), sems(chunks),
            *pair(2, chunks),
            sems(chunks), sems(BANDS - 1, chunks),
            sems(tables), sems(tables), one, one,
            *pair(2),
            *pair(2),
            *pair(2),
            sems(2), sems(SHARES // 2),
            one, one,
        ],
        compiler_params=pltpu.CompilerParams(
            collective_id=0, has_side_effects=True, vmem_limit_bytes=60 * 1024 * 1024
        ),
        cost_estimate=pl.CostEstimate(
            flops=6 * many * wide * 3 * width + 10 * many * 128 * width * 2,
            bytes_accessed=many * (2 * wide + width),
            transcendentals=many * 128 * 6,
        ),
    )(codes, cell_states, head_grads, proj_weights)
    return (input_grad, turned.T)


def normalize(states):
    widened = states.astype(jnp.float32)
    meansq = jnp.mean(widened * widened, axis=-1, keepdims=True)
    inverse = lax.rsqrt(meansq + EPSILON)
    scaled = widened * inverse
    return (scaled, inverse, scaled.astype(jnp.bfloat16))


def project(normed, weights):
    width = weights.shape[1] // 3
    flat = normed.reshape(-1, normed.shape[-1])
    mixed = jnp.dot(flat, weights, preferred_element_type=jnp.float32).astype(jnp.bfloat16)
    mixed = mixed.reshape(normed.shape[:-1] + (3 * width,))
    return (mixed[..., :width], mixed[..., width : 2 * width], mixed[..., 2 * width :])


def attend_back(query_rows, key_rows, value_rows, grad_rows, groups):
    shape = query_rows.shape
    split = shape[:-1] + (shape[-1] // HD, HD)
    query_five = query_rows.reshape(split)
    key_five = key_rows.reshape(split)
    value_five = value_rows.reshape(split)
    grad_five = grad_rows.reshape(split)
    scores = (
        jnp.einsum("bichd,bjchd->bchij", query_five, key_five, preferred_element_type=jnp.float32)
        * SCALE
    )
    header = lax.broadcasted_iota(jnp.int32, (shape[1], shape[1]), 1) == 0
    visible = (groups[:, :, :, None] == groups[:, :, None, :]) | header
    scores = jnp.where(visible[:, :, None], scores, -1e30)
    peak = jnp.max(scores, axis=-1, keepdims=True)
    expsc = jnp.exp(scores - peak)
    probs = expsc / jnp.sum(expsc, axis=-1, keepdims=True)
    probs_low = probs.astype(jnp.bfloat16)
    value_grad = jnp.einsum(
        "bchij,bichd->bjchd", probs_low, grad_five, preferred_element_type=jnp.float32
    ).astype(jnp.bfloat16)
    prob_grad = jnp.einsum(
        "bichd,bjchd->bchij", grad_five, value_five, preferred_element_type=jnp.float32
    )
    score_grad = probs * (prob_grad - jnp.sum(probs * prob_grad, axis=-1, keepdims=True))
    score_low = (score_grad * SCALE).astype(jnp.bfloat16)
    query_grad = jnp.einsum(
        "bchij,bjchd->bichd", score_low, key_five, preferred_element_type=jnp.float32
    ).astype(jnp.bfloat16)
    key_grad = jnp.einsum(
        "bchij,bichd->bjchd", score_low, query_five, preferred_element_type=jnp.float32
    ).astype(jnp.bfloat16)
    return (query_grad.reshape(shape), key_grad.reshape(shape), value_grad.reshape(shape))


def finish(scaled, inverse, normed, all_grads, weights):
    flat_norm = normed.reshape(-1, normed.shape[-1])
    flat_grad = all_grads.reshape(-1, all_grads.shape[-1])
    partial_w = lax.dot_general(
        flat_norm, flat_grad, (((0,), (0,)), ((), ())), preferred_element_type=jnp.float32
    )
    normed_grad = lax.dot_general(
        flat_grad, weights, (((1,), (1,)), ((), ())), preferred_element_type=jnp.float32
    )
    normed_grad = normed_grad.reshape(scaled.shape)
    coupling = jnp.mean(normed_grad * scaled, axis=-1, keepdims=True)
    state_grad = (inverse * (normed_grad - scaled * coupling)).astype(jnp.bfloat16)
    return (partial_w, state_grad)


def exchange_body(cell_states, head_grads, group_ids, proj_weights):
    scaled, inverse, normed = normalize(cell_states)
    query_rows, key_rows, value_rows = project(normed, proj_weights)
    query_cols, key_cols, value_cols, grad_cols = (
        lax.all_to_all(query_rows, "band", split_axis=2, concat_axis=1, tiled=True),
        lax.all_to_all(key_rows, "band", split_axis=2, concat_axis=1, tiled=True),
        lax.all_to_all(value_rows, "band", split_axis=2, concat_axis=1, tiled=True),
        lax.all_to_all(head_grads, "band", split_axis=2, concat_axis=1, tiled=True),
    )
    query_grad, key_grad, value_grad = attend_back(
        query_cols, key_cols, value_cols, grad_cols, group_ids
    )
    query_home, key_home, value_home = (
        lax.all_to_all(query_grad, "band", split_axis=1, concat_axis=2, tiled=True),
        lax.all_to_all(key_grad, "band", split_axis=1, concat_axis=2, tiled=True),
        lax.all_to_all(value_grad, "band", split_axis=1, concat_axis=2, tiled=True),
    )
    all_grads = jnp.concatenate((query_home, key_home, value_home), axis=-1)
    partial_w, input_grad = finish(scaled, inverse, normed, all_grads, proj_weights)
    shared = lax.psum_scatter(partial_w, "dp", scatter_dimension=1, tiled=True)
    weight_grad = lax.psum_scatter(shared, "band", scatter_dimension=0, tiled=True)
    return (input_grad, weight_grad)


def body(cell_states, head_grads, group_ids, proj_weights):
    halo = cell_states.shape[1] == BAND
    halo = halo and lax.axis_size("band") == BANDS and lax.axis_size("dp") == SHARES
    form = halo_body if halo else exchange_body
    return form(cell_states, head_grads, group_ids, proj_weights)


def solution(mesh):
    return jax.shard_map(
        body,
        mesh=mesh,
        in_specs=(
            P("dp", "band", None, None),
            P("dp", "band", None, None),
            P("dp", "band", None),
            P(),
        ),
        out_specs=(P("dp", "band", None, None), P("band", "dp")),
        check_vma=False,
    )
```

```python
import jax
import jax.numpy as jnp
from jax import lax
from jax.experimental import pallas as pl
from jax.experimental.pallas import tpu as pltpu
from jax.sharding import PartitionSpec as P

HD = 64
SCALE = 0.125
EPSILON = 1e-06
LOW = 4
HIGH = 3
BAND = 8
BANDS = 4
SHARES = 8
SLOTS = 1 + LOW + BAND + HIGH
SUB = 8
STEP = 32
CELLS = SLOTS * SUB
CHUNK = STEP
AHEAD = 2
LATE = 4
DEEP = 1024
F32 = jnp.float32
BF16 = jnp.bfloat16
MESH = pl.DeviceIdType.MESH


def dot(a, b, ca, cb):
    return lax.dot_general(a, b, (((ca,), (cb,)), ((), ())), preferred_element_type=F32)


def kernel(
    code_in, x_in, g_in, w_in, out, wout, x, g, w, w_turned,
    code, hx, lx, ux, lg, ug, from_high, from_low, from_head,
    normed_all, grads_t, grads_late, mixed, acc, half_send, half_recv,
    x_send, x_recv, kept, y_send, y_recv, z_send, z_recv, fin, fin_recv,
    code_ss, code_rs, halo_ss, halo_rs, head_ss, head_rs, back_ss, back_rs, top_ss, top_rs,
    load_x, load_g, load_w, load_h,
    half_ss, half_rs, x_ss, x_rs, y_ss, y_rs, z_ss, z_rs, fin_ss, fin_rs,
):
    tables, _, cols, wide = x_in.shape
    width = g_in.shape[-1]
    per_table = cols // CHUNK
    chunks = tables * per_table
    per_band = cols // BANDS // STEP
    band, share = lax.axis_index("band"), lax.axis_index("dp")
    core, side = lax.rem(band, 2), band // 2
    y, z = lax.rem(share, 2), share // 2
    sibling, across = side * 2 + 1 - core, (1 - side) * 2 + core

    def copy(src, dst, ss, rs, **where):
        return pltpu.make_async_remote_copy(
            src_ref=src, dst_ref=dst, send_sem=ss, recv_sem=rs, device_id=where, device_id_type=MESH
        )

    def loads(t):
        return (
            pltpu.make_async_copy(x_in.at[t], x.at[t], load_x.at[t]),
            pltpu.make_async_copy(g_in.at[t], g.at[t], load_g.at[t]),
        )

    weight_load = pltpu.make_async_copy(w_in, w, load_w)
    weight_load.start()
    for t in range(tables):
        for one in loads(t):
            one.start()

    barrier = pltpu.get_barrier_semaphore()
    for k in range(1, BANDS):
        pl.semaphore_signal(
            barrier, inc=1, device_id={"band": lax.rem(band + k, BANDS)}, device_id_type=MESH
        )
    pl.semaphore_signal(barrier, inc=1, device_id={"dp": z * 2 + 1 - y}, device_id_type=MESH)
    for k in range(1, SHARES // 2):
        other = lax.rem(z + k, SHARES // 2) * 2 + y
        pl.semaphore_signal(barrier, inc=1, device_id={"dp": other}, device_id_type=MESH)
    pl.semaphore_wait(barrier, BANDS + SHARES // 2 - 1)

    def place(c):
        return c // per_table, pl.ds(pl.multiple_of(lax.rem(c, per_table) * CHUNK, CHUNK), CHUNK)

    def code_copy(k):
        to = lax.rem(band + k, BANDS)
        return copy(code_in.at[to], code.at[band], code_ss.at[k - 1], code_rs.at[k - 1], band=to)

    def code_arrival(k):
        source = lax.rem(band + BANDS - k, BANDS)
        return copy(code_in.at[source], code.at[source], code_ss.at[k - 1], code_rs.at[k - 1], band=source)

    def head_copy(c, to):
        t, at = place(c)
        return copy(
            x_in.at[t, pl.ds(0, 1), at], hx.at[t, :, at], head_ss.at[to - 1, c], head_rs.at[c], band=to
        )

    def up_copies(c, to):
        t, at = place(c)
        rows = pl.ds(BAND - LOW, LOW)
        return (
            copy(x_in.at[t, rows, at], lx.at[t, :, at], halo_ss.at[0, c], halo_rs.at[0, c], band=to),
            copy(g_in.at[t, rows, at], lg.at[t, :, at], halo_ss.at[1, c], halo_rs.at[1, c], band=to),
        )

    def down_copies(c, to):
        t, at = place(c)
        rows = pl.ds(0, HIGH)
        return (
            copy(x_in.at[t, rows, at], ux.at[t, :, at], halo_ss.at[2, c], halo_rs.at[2, c], band=to),
            copy(g_in.at[t, rows, at], ug.at[t, :, at], halo_ss.at[3, c], halo_rs.at[3, c], band=to),
        )

    def back_low(c, to):
        t, at = place(c)
        return copy(lx.at[t, :, at], from_high.at[t, :, at], back_ss.at[0, c], back_rs.at[0, c], band=to)

    def back_high(c, to):
        t, at = place(c)
        return copy(ux.at[t, :, at], from_low.at[t, :, at], back_ss.at[1, c], back_rs.at[1, c], band=to)

    def back_head(c, source):
        t, at = place(c)
        return copy(
            hx.at[t, :, at], from_head.at[source - 1, t, :, at], top_ss.at[c], top_rs.at[source - 1, c],
            band=0,
        )

    has_low, has_high = band > 0, band < BANDS - 1

    for k in range(1, BANDS):
        code_copy(k).start()

    def send_chunk(c, carry):
        @pl.when(band == 0)
        def _():
            for to in range(1, BANDS):
                head_copy(c, to).start()

        @pl.when(has_high)
        def _():
            for one in up_copies(c, band + 1):
                one.start()

        @pl.when(has_low)
        def _():
            for one in down_copies(c, band - 1):
                one.start()

        return carry

    lax.fori_loop(0, AHEAD, send_chunk, 0)

    code[band] = code_in[band]

    @pl.when(band == 0)
    def _():
        for t in range(tables):
            own = pltpu.make_async_copy(x_in.at[t, pl.ds(0, 1)], hx.at[t], load_h)
            own.start()
            own.wait()

        lx[...] = jnp.zeros_like(lx)
        lg[...] = jnp.zeros_like(lg)

    @pl.when(band == BANDS - 1)
    def _():
        ux[...] = jnp.zeros_like(ux)
        ug[...] = jnp.zeros_like(ug)

    weight_load.wait()
    w_turned[...] = w[...].T

    for k in range(1, BANDS):
        code_arrival(k).wait_recv()

    lane = lax.broadcasted_iota(jnp.int32, (1, 128), 1)
    left = jnp.where(lane < HD, 1.0, 0.0).astype(BF16)
    right = jnp.where(lane < HD, 0.0, 1.0).astype(BF16)

    def split_heads(a):
        return jnp.concatenate((a * left, a * right), axis=0)

    def flat(parts):
        whole = jnp.concatenate(parts, axis=0).astype(F32)
        return jnp.concatenate(
            [whole[:, s : s + SUB].reshape(CELLS, whole.shape[-1]) for s in range(0, STEP, SUB)], axis=0
        )

    def norms(t, at):
        states = flat((hx[t, :, at], lx[t, :, at], x[t, :, at], ux[t, :, at]))
        inverse = lax.rsqrt(jnp.mean(states * states, axis=-1, keepdims=True) + EPSILON)
        return states * inverse, inverse

    def cells(c):
        return pl.ds(pl.multiple_of(c * SLOTS * STEP, SLOTS * STEP), SLOTS * STEP)

    def grads_of(c):
        t, at = place(c)
        at_step = lax.rem(c, per_table)
        scaled, inverse = norms(t, at)
        rows_all = cells(c)
        normed = scaled.astype(BF16)
        normed_all[rows_all] = normed
        mixed[...] = dot(normed, w[...], 1, 0).astype(BF16)
        cotangent = flat((jnp.zeros((1, STEP, width), BF16), lg[t, :, at], g[t, :, at], ug[t, :, at]))
        cotangent = cotangent.astype(BF16)
        marks = code[at_step // per_band, t, lax.rem(at_step, per_band)]
        biases = []
        for s in range(STEP // SUB):
            query_code = marks[s : s + 1]
            key_code = jnp.broadcast_to(marks[STEP // SUB + s : STEP // SUB + s + 1], (CELLS, CELLS)).T
            row = lax.broadcasted_iota(jnp.int32, (CELLS, CELLS), 0)
            visible = (key_code == query_code) | (row == (query_code >> 3))
            biases.append(jnp.where(visible, 0.0, -1e30).astype(F32))
        units = [(s, p) for s in range(STEP // SUB) for p in range(width // 128)]

        def part(kind, s, p):
            start = kind * width + 128 * p
            return mixed[s * CELLS : (s + 1) * CELLS, start : start + 128]

        scale = jnp.asarray(SCALE, BF16)
        grad = [cotangent[s * CELLS : (s + 1) * CELLS, 128 * p : 128 * p + 128] for s, p in units]
        query = [part(0, s, p) * scale for s, p in units]
        scores = [
            dot(split_heads(part(1, s, p)), q, 1, 1).reshape(2, CELLS, CELLS)
            for (s, p), q in zip(units, query)
        ]
        prob_grad = [
            dot(split_heads(part(2, s, p)), d, 1, 1).reshape(2, CELLS, CELLS)
            for (s, p), d in zip(units, grad)
        ]
        all_grads = {}
        for n, (s, p) in enumerate(units):
            masked = scores[n] + biases[s][None]
            peak = jnp.maximum(jnp.max(masked, axis=1, keepdims=True), -1e29)
            expsc = jnp.exp(masked - peak)
            total = jnp.maximum(jnp.sum(expsc, axis=1, keepdims=True), 1.0)
            probs = expsc * (1.0 / total)
            delta = jnp.sum(probs * prob_grad[n], axis=1, keepdims=True)
            score_low = (probs * (prob_grad[n] - delta)).astype(BF16)
            probs_low = probs.astype(BF16)
            value_grad = dot(
                jnp.concatenate((probs_low[0], probs_low[1]), axis=1), split_heads(grad[n]), 1, 0
            )
            key_grad = dot(
                jnp.concatenate((score_low[0], score_low[1]), axis=1), split_heads(query[n]), 1, 0
            )
            query_grad = dot(
                score_low.reshape(2 * CELLS, CELLS), split_heads(part(1, s, p) * scale), 0, 0
            )
            all_grads[s, 0, p] = query_grad.astype(BF16)
            all_grads[s, 1, p] = key_grad.astype(BF16)
            all_grads[s, 2, p] = value_grad.astype(BF16)
        joined = jnp.concatenate(
            [
                jnp.concatenate([all_grads[s, k, p] for k in range(3) for p in range(width // 128)], axis=1)
                for s in range(STEP // SUB)
            ],
            axis=0,
        )
        turned = joined.T
        grads_t[:, rows_all] = turned
        return scaled, inverse, joined

    def finish(c, scaled, inverse, joined):
        t, at = place(c)
        normed_grad = dot(joined, w_turned[...], 1, 0)
        coupling = jnp.mean(normed_grad * scaled, axis=-1, keepdims=True)
        result = inverse * (normed_grad - scaled * coupling)
        pieces = [result[s * CELLS : (s + 1) * CELLS].reshape(SLOTS, SUB, wide) for s in range(STEP // SUB)]
        result = jnp.concatenate(pieces, axis=1).astype(BF16)
        hx[t, :, at] = result[:1]
        lx[t, :, at] = result[1 : 1 + LOW]
        out[t, :, at] = result[1 + LOW : 1 + LOW + BAND]
        ux[t, :, at] = result[1 + LOW + BAND :]

        @pl.when(has_low)
        def _():
            back_low(c, band - 1).start()

        @pl.when(has_high)
        def _():
            back_high(c, band + 1).start()

        for source in range(1, BANDS):

            @pl.when(band == source)
            def _():
                back_head(c, source).start()

    def arrive(c):
        @pl.when(lax.rem(c, per_table) == 0)
        def _():
            for one in loads(c // per_table):
                one.wait()

        @pl.when(band > 0)
        def _():
            head_copy(c, 1).wait_recv()

        @pl.when(has_low)
        def _():
            for one in up_copies(c, 0):
                one.wait_recv()

        @pl.when(has_high)
        def _():
            for one in down_copies(c, 0):
                one.wait_recv()

        @pl.when(c + AHEAD < chunks)
        def _():
            send_chunk(c + AHEAD, 0)

    early = chunks - LATE

    def work_early(c, carry):
        arrive(c)
        finish(c, *grads_of(c))
        return carry

    def work_late(c, carry):
        arrive(c)
        grads_late[cells(c - early)] = grads_of(c)[2]
        return carry

    def end_late(c, carry):
        t, at = place(c)
        scaled, inverse = norms(t, at)
        finish(c, scaled, inverse, grads_late[cells(c - early)])
        return carry

    def late(n):
        lax.fori_loop(early + n, early + n + 1, end_late, 0)

    lax.fori_loop(0, early, work_early, 0)
    lax.fori_loop(early, chunks, work_late, 0)

    total_rows = normed_all.shape[0]
    block = 3 * width // SHARES
    rows_half = SHARES // 2 * block
    mine = pl.ds(pl.multiple_of(core * rows_half, 16), rows_half)
    theirs = pl.ds(pl.multiple_of((1 - core) * rows_half, 16), rows_half)

    def product(n, which, begin, end):
        lanes = pl.ds(pl.multiple_of(which * (wide // 2), 128), wide // 2)

        def deep(i, carry):
            at = pl.ds(pl.multiple_of(i * DEEP, DEEP), DEEP)
            acc[n] += dot(grads_t[:, at], normed_all[at, lanes], 1, 0)
            return carry

        lax.fori_loop(begin, end, deep, 0)

    def half_copy(n):
        return copy(half_send.at[n], half_recv.at[n], half_ss.at[n], half_rs.at[n], band=sibling)

    def x_copy(j):
        return copy(x_send.at[j], x_recv.at[j], x_ss.at[j], x_rs.at[j], band=across)

    def piece(j):
        return pl.ds(pl.multiple_of(core * rows_half + j * (2 * block), 16), 2 * block)

    deeps = total_rows // DEEP
    acc[...] = jnp.zeros_like(acc)
    product(0, 1 - side, 0, deeps)
    half_send[0] = acc[0, theirs, :].astype(BF16)
    half_copy(0).start()
    product(1, side, 0, 1)
    half_copy(0).wait_recv()
    for j in range(2):
        partner = half_recv[0, 2 * block * j : 2 * block * (j + 1)].astype(F32)
        x_send[j] = (acc[0, piece(j), :] + partner).astype(BF16)
        x_copy(j).start()
    product(1, side, 1, deeps)
    half_send[1] = acc[1, theirs, :].astype(BF16)
    half_copy(1).start()

    def y_copy(j):
        return copy(y_send.at[j], y_recv.at[j], y_ss.at[j], y_rs.at[j], dp=z * 2 + 1 - y)

    late(0)
    half_copy(1).wait_recv()
    for j in range(2):
        x_copy(j).wait_recv()
        whole = acc[1, piece(j), :] + half_recv[1, 2 * block * j : 2 * block * (j + 1)].astype(F32)
        whole = (whole + x_recv[j].astype(F32)).reshape(2, block, wide // 2)
        kept[j] = jnp.where(y == 0, whole[0], whole[1])
        y_send[j] = jnp.where(y == 0, whole[1], whole[0]).astype(BF16)
        y_copy(j).start()

    def z_copy(j, source):
        return copy(z_send.at[j], z_recv.at[source], z_ss.at[j], z_rs.at[source], dp=(2 * core + j) * 2 + y)

    zs = SHARES // 2
    late(1)
    for j in range(2):
        y_copy(j).wait_recv()
        kept[j] += y_recv[j].astype(F32)
        z_send[j] = kept[j].astype(BF16)
        for source in range(zs):

            @pl.when((z == source) & (2 * core + j != z))
            def _():
                z_copy(j, source).start()

    fin_copy = copy(fin, fin_recv, fin_ss, fin_rs, band=sibling)
    holder = z // 2 == core

    def emit(full):
        half = wide // 4
        wout[...] = jnp.where(core == 0, full[:, :half], full[:, half:])

    late(2)

    @pl.when(holder)
    def _():
        fin[...] = jnp.where(lax.rem(z, 2) == 0, kept[0], kept[1])
        for source in range(zs):

            @pl.when(z != source)
            def _():
                z_copy(0, source).wait_recv()
                fin[...] += z_recv[source].astype(F32)

        fin_copy.start()
        emit(fin[...])

    late(3)

    def merge_chunk(c, carry):
        t, at = place(c)

        @pl.when(has_high)
        def _():
            back_low(c, 0).wait_recv()
            rows = pl.ds(BAND - LOW, LOW)
            out[t, rows, at] = (out[t, rows, at].astype(F32) + from_high[t, :, at].astype(F32)).astype(BF16)

        @pl.when(has_low)
        def _():
            back_high(c, 0).wait_recv()
            rows = pl.ds(0, HIGH)
            out[t, rows, at] = (out[t, rows, at].astype(F32) + from_low[t, :, at].astype(F32)).astype(BF16)

        @pl.when(band == 0)
        def _():
            top = out[t, 0:1, at].astype(F32) + hx[t, :, at].astype(F32)
            for source in range(1, BANDS):
                back_head(c, source).wait_recv()
                top = top + from_head[source - 1, t, :, at].astype(F32)
            out[t, 0:1, at] = top.astype(BF16)

        return carry

    lax.fori_loop(0, chunks, merge_chunk, 0)

    @pl.when(holder)
    def _():
        fin_copy.wait_send()

    @pl.when(jnp.logical_not(holder))
    def _():
        fin_copy.wait_recv()
        emit(fin_recv[...])

    for k in range(1, BANDS):
        code_copy(k).wait_send()

    def drain(c, carry):
        @pl.when(band == 0)
        def _():
            for to in range(1, BANDS):
                head_copy(c, to).wait_send()

        @pl.when(has_high)
        def _():
            for one in up_copies(c, band + 1):
                one.wait_send()
            back_high(c, band + 1).wait_send()

        @pl.when(has_low)
        def _():
            for one in down_copies(c, band - 1):
                one.wait_send()
            back_low(c, band - 1).wait_send()
            back_head(c, 1).wait_send()

        return carry

    lax.fori_loop(0, chunks, drain, 0)
    half_copy(0).wait_send()
    half_copy(1).wait_send()
    for j in range(2):
        x_copy(j).wait_send()
        y_copy(j).wait_send()

        @pl.when(2 * core + j != z)
        def _():
            z_copy(j, 0).wait_send()


def group_codes(group_ids):
    bands = group_ids.reshape(group_ids.shape[:2] + (BANDS, BAND))
    first = bands[..., :1]
    following = jnp.pad(first[:, :, 1:], ((0, 0), (0, 0), (0, 1), (0, 0)), constant_values=-1)
    tail = bands == following
    head = bands == first
    below = jnp.sum(tail, axis=-1, keepdims=True)
    above = jnp.sum(head, axis=-1, keepdims=True)
    above_next = jnp.pad(above[:, :, 1:], ((0, 0), (0, 0), (0, 1), (0, 0)))
    below_last = jnp.pad(below[:, :, :-1], ((0, 0), (0, 0), (1, 0), (0, 0)))
    goes_up = tail & (below <= above_next)
    goes_down = head & (below_last > above)
    owner = jnp.arange(BANDS)[:, None] + goes_up.astype(jnp.int32) - goes_down.astype(jnp.int32)
    return (bands + 8 * owner).astype(jnp.int32).reshape(group_ids.shape)


def slot_codes(codes, band):
    tables, cols, rows = codes.shape
    padded = jnp.pad(codes, ((0, 0), (0, 0), (LOW, HIGH)), constant_values=-8)
    near = padded[:, :, band * BAND : band * BAND + LOW + BAND + HIGH]
    row = band * BAND - LOW + jnp.arange(LOW + BAND + HIGH)
    alive = (near >> 3) == band
    mark = (jnp.arange(cols) % SUB)[None, :, None] * 8 + (near & 7)
    query = jnp.where(alive, mark, -1)
    key = jnp.where(alive & (row != 0), mark, -2)

    def order(values, header):
        values = jnp.pad(values, ((0, 0), (0, 0), (1, 0)), constant_values=header)
        values = values.reshape(tables, cols // STEP, STEP // SUB, SUB, SLOTS)
        return values.transpose(0, 1, 2, 4, 3).reshape(tables, cols // STEP, STEP // SUB, CELLS)

    return jnp.concatenate((order(query, -1), order(key, -2)), axis=2).astype(jnp.int32)


def halo_body(cell_states, head_grads, group_ids, proj_weights):
    tables, _, cols, wide = cell_states.shape
    width = head_grads.shape[-1]
    codes = group_codes(group_ids)
    codes = jnp.stack([slot_codes(codes, b) for b in range(BANDS)])
    chunks = tables * cols // CHUNK
    many = SLOTS * tables * cols
    block = 3 * width // SHARES
    rows_half, lanes = 3 * width // 2, wide // 2
    halo = lambda rows, features: pltpu.VMEM((tables, rows, cols, features), BF16)
    sems = lambda *shape: pltpu.SemaphoreType.DMA(shape)
    pair = lambda *shape: [sems(*shape), sems(*shape)]
    one = pltpu.SemaphoreType.DMA
    vmem = pl.BlockSpec(memory_space=pltpu.VMEM)
    input_grad, turned = pl.pallas_call(
        kernel,
        in_specs=[vmem] + [pl.BlockSpec(memory_space=pl.ANY)] * 3,
        out_specs=[vmem] * 2,
        out_shape=[
            jax.ShapeDtypeStruct(cell_states.shape, BF16),
            jax.ShapeDtypeStruct((block, wide // BANDS), F32),
        ],
        scratch_shapes=[
            pltpu.VMEM(cell_states.shape, BF16),
            pltpu.VMEM(head_grads.shape, BF16),
            pltpu.VMEM(proj_weights.shape, BF16),
            pltpu.VMEM((3 * width, wide), BF16),
            pltpu.VMEM(codes.shape, jnp.int32),
            halo(1, wide), halo(LOW, wide), halo(HIGH, wide), halo(LOW, width), halo(HIGH, width),
            halo(LOW, wide), halo(HIGH, wide),
            pltpu.VMEM((BANDS - 1, tables, 1, cols, wide), BF16),
            pltpu.VMEM((many, wide), BF16),
            pltpu.VMEM((3 * width, many), BF16),
            pltpu.VMEM((LATE * SLOTS * STEP, 3 * width), BF16),
            pltpu.VMEM((SLOTS * STEP, 3 * width), BF16),
            pltpu.VMEM((2, 3 * width, lanes), F32),
            pltpu.VMEM((2, rows_half, lanes), BF16),
            pltpu.VMEM((2, rows_half, lanes), BF16),
            pltpu.VMEM((2, 2 * block, lanes), BF16),
            pltpu.VMEM((2, 2 * block, lanes), BF16),
            pltpu.VMEM((2, block, lanes), F32),
            pltpu.VMEM((2, block, lanes), BF16),
            pltpu.VMEM((2, block, lanes), BF16),
            pltpu.VMEM((2, block, lanes), BF16),
            pltpu.VMEM((SHARES // 2, block, lanes), BF16),
            pltpu.VMEM((block, lanes), F32),
            pltpu.VMEM((block, lanes), F32),
            *pair(BANDS - 1),
            *pair(4, chunks),
            sems(BANDS - 1, chunks), sems(chunks),
            *pair(2, chunks),
            sems(chunks), sems(BANDS - 1, chunks),
            sems(tables), sems(tables), one, one,
            *pair(2),
            *pair(2),
            *pair(2),
            sems(2), sems(SHARES // 2),
            one, one,
        ],
        compiler_params=pltpu.CompilerParams(
            collective_id=0, has_side_effects=True, vmem_limit_bytes=60 * 1024 * 1024
        ),
        cost_estimate=pl.CostEstimate(
            flops=6 * many * wide * 3 * width + 10 * many * 128 * width * 2,
            bytes_accessed=many * (2 * wide + width),
            transcendentals=many * 128 * 6,
        ),
    )(codes, cell_states, head_grads, proj_weights)
    return (input_grad, turned.T)


def normalize(states):
    widened = states.astype(jnp.float32)
    meansq = jnp.mean(widened * widened, axis=-1, keepdims=True)
    inverse = lax.rsqrt(meansq + EPSILON)
    scaled = widened * inverse
    return (scaled, inverse, scaled.astype(jnp.bfloat16))


def project(normed, weights):
    width = weights.shape[1] // 3
    flat = normed.reshape(-1, normed.shape[-1])
    mixed = jnp.dot(flat, weights, preferred_element_type=jnp.float32).astype(jnp.bfloat16)
    mixed = mixed.reshape(normed.shape[:-1] + (3 * width,))
    return (mixed[..., :width], mixed[..., width : 2 * width], mixed[..., 2 * width :])


def attend_back(query_rows, key_rows, value_rows, grad_rows, groups):
    shape = query_rows.shape
    split = shape[:-1] + (shape[-1] // HD, HD)
    query_five = query_rows.reshape(split)
    key_five = key_rows.reshape(split)
    value_five = value_rows.reshape(split)
    grad_five = grad_rows.reshape(split)
    scores = (
        jnp.einsum("bichd,bjchd->bchij", query_five, key_five, preferred_element_type=jnp.float32)
        * SCALE
    )
    header = lax.broadcasted_iota(jnp.int32, (shape[1], shape[1]), 1) == 0
    visible = (groups[:, :, :, None] == groups[:, :, None, :]) | header
    scores = jnp.where(visible[:, :, None], scores, -1e30)
    peak = jnp.max(scores, axis=-1, keepdims=True)
    expsc = jnp.exp(scores - peak)
    probs = expsc / jnp.sum(expsc, axis=-1, keepdims=True)
    probs_low = probs.astype(jnp.bfloat16)
    value_grad = jnp.einsum(
        "bchij,bichd->bjchd", probs_low, grad_five, preferred_element_type=jnp.float32
    ).astype(jnp.bfloat16)
    prob_grad = jnp.einsum(
        "bichd,bjchd->bchij", grad_five, value_five, preferred_element_type=jnp.float32
    )
    score_grad = probs * (prob_grad - jnp.sum(probs * prob_grad, axis=-1, keepdims=True))
    score_low = (score_grad * SCALE).astype(jnp.bfloat16)
    query_grad = jnp.einsum(
        "bchij,bjchd->bichd", score_low, key_five, preferred_element_type=jnp.float32
    ).astype(jnp.bfloat16)
    key_grad = jnp.einsum(
        "bchij,bichd->bjchd", score_low, query_five, preferred_element_type=jnp.float32
    ).astype(jnp.bfloat16)
    return (query_grad.reshape(shape), key_grad.reshape(shape), value_grad.reshape(shape))


def finish(scaled, inverse, normed, all_grads, weights):
    flat_norm = normed.reshape(-1, normed.shape[-1])
    flat_grad = all_grads.reshape(-1, all_grads.shape[-1])
    partial_w = lax.dot_general(
        flat_norm, flat_grad, (((0,), (0,)), ((), ())), preferred_element_type=jnp.float32
    )
    normed_grad = lax.dot_general(
        flat_grad, weights, (((1,), (1,)), ((), ())), preferred_element_type=jnp.float32
    )
    normed_grad = normed_grad.reshape(scaled.shape)
    coupling = jnp.mean(normed_grad * scaled, axis=-1, keepdims=True)
    state_grad = (inverse * (normed_grad - scaled * coupling)).astype(jnp.bfloat16)
    return (partial_w, state_grad)


def exchange_body(cell_states, head_grads, group_ids, proj_weights):
    scaled, inverse, normed = normalize(cell_states)
    query_rows, key_rows, value_rows = project(normed, proj_weights)
    query_cols, key_cols, value_cols, grad_cols = (
        lax.all_to_all(query_rows, "band", split_axis=2, concat_axis=1, tiled=True),
        lax.all_to_all(key_rows, "band", split_axis=2, concat_axis=1, tiled=True),
        lax.all_to_all(value_rows, "band", split_axis=2, concat_axis=1, tiled=True),
        lax.all_to_all(head_grads, "band", split_axis=2, concat_axis=1, tiled=True),
    )
    query_grad, key_grad, value_grad = attend_back(
        query_cols, key_cols, value_cols, grad_cols, group_ids
    )
    query_home, key_home, value_home = (
        lax.all_to_all(query_grad, "band", split_axis=1, concat_axis=2, tiled=True),
        lax.all_to_all(key_grad, "band", split_axis=1, concat_axis=2, tiled=True),
        lax.all_to_all(value_grad, "band", split_axis=1, concat_axis=2, tiled=True),
    )
    all_grads = jnp.concatenate((query_home, key_home, value_home), axis=-1)
    partial_w, input_grad = finish(scaled, inverse, normed, all_grads, proj_weights)
    shared = lax.psum_scatter(partial_w, "dp", scatter_dimension=1, tiled=True)
    weight_grad = lax.psum_scatter(shared, "band", scatter_dimension=0, tiled=True)
    return (input_grad, weight_grad)


def body(cell_states, head_grads, group_ids, proj_weights):
    halo = cell_states.shape[1] == BAND
    halo = halo and lax.axis_size("band") == BANDS and lax.axis_size("dp") == SHARES
    form = halo_body if halo else exchange_body
    return form(cell_states, head_grads, group_ids, proj_weights)


def solution(mesh):
    return jax.shard_map(
        body,
        mesh=mesh,
        in_specs=(
            P("dp", "band", None, None),
            P("dp", "band", None, None),
            P("dp", "band", None),
            P(),
        ),
        out_specs=(P("dp", "band", None, None), P("band", "dp")),
        check_vma=False,
    )
```
